32 devices in a mesh: parts: 2 (over x), xfer: 16 (over z, y, core).
Axes of the slice: x: 2, y: 2, z: 4, core: 2. Of those that a mesh axis runs over, the one named last changes fastest.
Arguments:
- hidden_in: bfloat16 [64, 2, 8192], P(('parts', 'xfer')), parts along dimension 0, may hold values from -6 to 6
- latent_cache: bfloat16 [32, 16384, 512], P('parts', 'xfer'), parts along dimension 0, may hold values from -1600 to 1600
- lengths: int32 [32], P('parts'), parts along dimension 0, may hold values from 1 to 16384, 131072 in all
- placement: int32 [32], P('parts'), parts along dimension 0, may hold values from 0 to 15, each once
- w_query: bfloat16 [8192, 8192], P(None, 'xfer'), may hold values from -0.0625 to 0.0625
- w_down: bfloat16 [8192, 512], P(None, 'xfer'), may hold values from -0.0625 to 0.0625
- up_key: bfloat16 [256, 1024], replicated, may hold values from -0.5 to 0.5
- up_value: bfloat16 [256, 1024], replicated, may hold values from -0.375 to 0.375
- w_out: bfloat16 [8192, 8192], P('xfer'), may hold values from -0.0625 to 0.0625
Outputs:
- attended: bfloat16 [64, 2, 8192], P(('parts', 'xfer')), parts along dimension 0
The draws below stay inside these ranges and needn't reach their ends.
There are 2 independent parts, one for each index of `parts`. The reference program is written for one: setup_inputs(seed, part) draws one part's arguments, and reference() takes and returns one part's arrays. A program takes and returns all parts, laid end to end along the dimension named above; an argument that names none is the same for every part. Nothing has to cross between parts.
Inputs may be any that keep to these rules, and one draw needn't show every extreme that they name: `lengths`: prompt length of each request; some request has exactly 16384 positions. Each request appears once; request placement[j] is decoded by devices j * 1 to (j + 1) - 1, each holding 2 of its samples in order.
All inputs are finite; a program needn't handle non-finite values.
Results may differ from the reference program's by a relative error of at most 0.012.
The reference program's roundings to bfloat16 on the way count: a program that leaves them out, or rounds other values in their place, can miss the bound.
Values may be sent and summed in bfloat16 or wider, within the bound.
A program may use at most 192 MiB of HBM per device.

```python
import math
import jax
import jax.numpy as jnp
import numpy as np
from jax import lax

D = 8192
HEADS = 64
KVH = 8
HD = 128
RANK = 256
R = 16
LMAX = 16384
SAMPLES = 2
ROWS = 32


def draw_latent_cache(key, part):
    key = jax.random.fold_in(key, 11)
    first_key, second_key, third_key = jax.random.split(key, 3)
    shape = (R, LMAX, 2 * RANK)
    base = jax.random.truncated_normal(first_key, -6.0, 6.0, shape, jnp.float32)
    strength = jnp.exp(jax.random.uniform(second_key, (R,), jnp.float32, math.log(60.0), math.log(200.0)))
    chosen = jax.random.permutation(third_key, R) < max(R // 4, 1)
    leading = base[:, 0, :RANK] * strength[:, None]
    follower = leading * 1.01
    where_pos = jnp.arange(LMAX, dtype=jnp.int32)
    at_first = chosen[:, None, None] & (where_pos == 0)[None, :, None]
    at_second = chosen[:, None, None] & (where_pos == 1)[None, :, None]
    key_part = base[..., :RANK]
    key_part = jnp.where(at_first, leading[:, None, :], key_part)
    key_part = jnp.where(at_second, follower[:, None, :], key_part)
    return jnp.concatenate([key_part, base[..., RANK:]], axis=-1).astype(jnp.bfloat16)


def level_of(rng, extent, pieces, low, largest):
    def one(axis_at, parts):
        heights = jax.random.uniform(jax.random.fold_in(jax.random.fold_in(rng, 6), axis_at), (parts,), jnp.float32, low / len(pieces), largest / len(pieces))
        return jnp.repeat(jnp.exp(heights), extent[axis_at] // parts).reshape((-1,) + (1,) * (len(extent) - axis_at - 1))

    loudness = one(*pieces[0])
    for cut in pieces[1:]:
        loudness = loudness * one(*cut)
    return loudness


def profile(amount, total, reach, slope):
    portions = [(1 << 20) // math.isqrt(standing ** slope) + 1 for standing in range(2, amount + 1)]
    surplus, counts = total - reach - (amount - 1), [1] * (amount - 1)
    while surplus > 0:
        candidates = [i for i in range(amount - 1) if counts[i] < reach]
        whole, budget = sum([portions[i] for i in candidates]), surplus
        for i in candidates:
            extra = min(reach - counts[i], max(1, budget * portions[i] // whole), surplus)
            counts[i] = counts[i] + extra
            surplus = surplus - extra
    return np.array([reach] + counts)


def uneven(own_key, number_of, total, reach, slope):
    if number_of == 2:
        one = jax.random.randint(own_key, (), max(1, total - reach), min(reach, total - 1) + 1)
        return jnp.stack([one, total - one])
    sizes = jnp.asarray(profile(number_of, total, reach, slope), jnp.int32)
    pairs = (number_of - 1) // 2
    donor, receiver = sizes[1:1 + 2 * pairs:2], sizes[2:2 + 2 * pairs:2]
    slack = jnp.minimum(donor - 1, reach - receiver)
    passed = jax.random.randint(jax.random.fold_in(own_key, 1), (pairs,), 0, 1 << 20) % (slack + 1)
    sizes = sizes.at[1:1 + 2 * pairs:2].set(donor - passed).at[2:2 + 2 * pairs:2].set(receiver + passed)
    return sizes[jax.random.permutation(jax.random.fold_in(own_key, 2), number_of)]


def gaussian(own_key, shape, scale, limit, shards=(), held_as=jnp.bfloat16):
    drawn = scale * jax.random.normal(own_key, shape, jnp.float32)
    if shards:
        drawn = drawn * level_of(own_key, shape, shards, -0.22, 0.18)
    return jnp.clip(drawn, -limit, limit).astype(held_as)


def setup_inputs(seed: int = 0, part: int = 0) -> dict:
    streams_of = jax.random.split(jax.random.key(seed), 10)
    part_splits = jax.random.split(jax.random.fold_in(streams_of[9], part), 10)
    return {
        "hidden_in": gaussian(part_splits[0], (ROWS, 2, D), 1.0, 6.0, ((0, 16),)),
        "latent_cache": draw_latent_cache(jax.random.fold_in(jax.random.fold_in(streams_of[9], part), 71), part),
        "lengths": uneven(part_splits[2], R, R * LMAX // 2, LMAX, 2).astype(jnp.int32),
        "placement": jax.random.permutation(part_splits[3], R).astype(jnp.int32),
        "w_query": gaussian(streams_of[4], (D, HEADS * HD), D ** -0.5, 0.0625, ((1, 16),)),
        "w_down": gaussian(streams_of[5], (D, 2 * RANK), D ** -0.5, 0.0625, ((1, 16),)),
        "up_key": gaussian(streams_of[6], (RANK, KVH * HD), HD ** -0.5, 0.5),
        "up_value": gaussian(streams_of[7], (RANK, KVH * HD), RANK ** -0.5, 0.375),
        "w_out": gaussian(streams_of[8], (HEADS * HD, D), (HEADS * HD) ** -0.5, 0.0625, ((0, 16),)),
    }


def expand(up):
    return jnp.repeat(up.reshape(RANK, KVH, HD), HEADS // KVH, axis=1).astype(jnp.float32)


def reference(hidden_in, latent_cache, lengths, placement, w_query, w_down, up_key, up_value, w_out):
    highest = lax.Precision.HIGHEST
    offsets = jnp.arange(SAMPLES, dtype=jnp.int32)
    row_index = (placement[:, None] * SAMPLES + offsets[None, :]).reshape(-1).astype(jnp.int32)
    ordered = hidden_in[row_index].reshape(-1, D)
    query = jnp.dot(ordered, w_query, preferred_element_type=jnp.float32).astype(jnp.bfloat16)
    fresh = jnp.dot(ordered, w_down, preferred_element_type=jnp.float32).astype(jnp.bfloat16)
    query = lax.optimization_barrier(query).reshape(R, SAMPLES, 2, HEADS, HD)
    fresh = lax.optimization_barrier(fresh).reshape(R, SAMPLES, 2, 2 * RANK)
    key_up = expand(up_key)
    value_up = expand(up_value)
    scale = HD ** -0.5
    steps_mask = jnp.tril(jnp.ones((2, 2), dtype=bool))
    positions = jnp.arange(LMAX, dtype=jnp.int32)

    def one(item):
        queries, own, request = item
        cache = latent_cache[request].astype(jnp.float32)
        length = lengths[request]
        absorbed = jnp.einsum('sthd,rhd->sthr', queries.astype(jnp.float32), key_up, precision=highest)
        far = jnp.einsum('sthr,lr->sthl', absorbed, cache[:, :RANK], precision=highest) * scale
        far = jnp.where((positions < length)[None, None, None, :], far, -1e30)
        near = jnp.einsum('sthr,sur->sthu', absorbed, own[..., :RANK].astype(jnp.float32), precision=highest) * scale
        near = jnp.where(steps_mask[None, :, None, :], near, -1e30)
        top = jnp.maximum(jnp.max(far, -1), jnp.max(near, -1))
        far_w = jnp.exp(far - top[..., None])
        near_w = jnp.exp(near - top[..., None])
        total = jnp.sum(far_w, -1) + jnp.sum(near_w, -1)
        far_b = lax.optimization_barrier(far_w.astype(jnp.bfloat16)).astype(jnp.float32)
        near_b = lax.optimization_barrier(near_w.astype(jnp.bfloat16)).astype(jnp.float32)
        latent_out = jnp.einsum('sthl,lr->sthr', far_b, cache[:, RANK:], precision=highest)
        latent_out = latent_out + jnp.einsum('sthu,sur->sthr', near_b, own[..., RANK:].astype(jnp.float32), precision=highest)
        latent_out = latent_out / total[..., None]
        return jnp.einsum('sthr,rhd->sthd', latent_out, value_up, precision=highest).astype(jnp.bfloat16)

    head_out = lax.map(one, (query, fresh, placement))
    head_out = head_out.reshape(ROWS * 2, HEADS * HD)
    attended = jnp.dot(head_out, w_out, preferred_element_type=jnp.float32).astype(jnp.bfloat16)
    return attended.reshape(ROWS, 2, D)
```

```python
import functools

import jax
import jax.numpy as jnp
from jax import lax
from jax.experimental import pallas as pl
from jax.experimental.pallas import tpu as pltpu
from jax.sharding import PartitionSpec as P

HEADS = 64
KVH = 8
HD = 128
R = 16
NEG = -1e30
BF = jnp.bfloat16
F32 = jnp.float32


def dot_nt(a, b):
    return lax.dot_general(a, b, (((1,), (1,)), ((), ())), preferred_element_type=F32)


def flash_kernel(hl, lengths_ref, where_ref, q_ref, fresh_ref, cache_ref, upk_ref, upv_ref,
                 o_ref, lse_ref, hi_ref, lo_ref, lat_ref):
    ndevs, _, per, _ = q_ref.shape
    rank = upk_ref.shape[1]
    rows = ndevs * per
    each = ndevs // KVH
    positions = cache_ref.shape[1]
    req = pl.program_id(0)

    @pl.when(req == 0)
    def _():
        for g in range(KVH):
            qg = q_ref[g * each:(g + 1) * each].reshape(each * R * per, HD)
            a = jnp.dot(qg, upk_ref[g * HD:(g + 1) * HD], preferred_element_type=F32)
            a = a * (HD ** -0.5)
            hi = a.astype(BF)
            lo = (a - hi.astype(F32)).astype(BF)
            hi_ref[g * each:(g + 1) * each] = hi.reshape(each, R, per, rank)
            lo_ref[g * each:(g + 1) * each] = lo.reshape(each, R, per, rank)

    first = where_ref[0] * positions
    seen = lengths_ref[req] - first
    last = where_ref[0] == where_ref[1] - 1

    qh = hi_ref[:, pl.ds(req, 1)].reshape(rows, rank)
    ql = lo_ref[:, pl.ds(req, 1)].reshape(rows, rank)
    key = cache_ref[0, :, :rank]
    val = cache_ref[0, :, rank:]
    s = dot_nt(qh, key) + dot_nt(ql, key)
    pos = lax.broadcasted_iota(jnp.int32, s.shape, 1)
    s = jnp.where(pos < seen, s, NEG)
    fk = fresh_ref[0, :, :rank]
    fv = fresh_ref[0, :, rank:]
    n = dot_nt(qh, fk) + dot_nt(ql, fk)
    row = lax.broadcasted_iota(jnp.int32, n.shape, 0) % per
    col = lax.broadcasted_iota(jnp.int32, n.shape, 1)
    rs, rt = row // (2 * hl), (row // hl) % 2
    ok = (rs == col // 2) & (col % 2 <= rt) & last
    n = jnp.where(ok, n, NEG)
    top = jnp.maximum(jnp.max(s, axis=1, keepdims=True), jnp.max(n, axis=1, keepdims=True))
    p = jnp.exp(s - top)
    pn = jnp.exp(n - top)
    total = jnp.sum(p, axis=1, keepdims=True) + jnp.sum(pn, axis=1, keepdims=True)
    acc = jnp.dot(p.astype(BF), val, preferred_element_type=F32)
    acc = acc + jnp.dot(pn.astype(BF), fv, preferred_element_type=F32)
    lat_ref[:, pl.ds(req, 1)] = (acc / total).astype(BF).reshape(ndevs, 1, per, rank)
    lse_ref[0] = jnp.broadcast_to(top + jnp.log(total), (rows, 128))

    @pl.when(req == R - 1)
    def _():
        for g in range(KVH):
            lg = lat_ref[g * each:(g + 1) * each].reshape(each * R * per, rank)
            o = jnp.dot(lg, upv_ref[:, g * HD:(g + 1) * HD], preferred_element_type=F32)
            o_ref[g * each:(g + 1) * each] = o.astype(BF).reshape(each, R, per, HD)


def flash(q, fresh, cache, lengths, upk, upv, mine, ndevs, hl):
    _, _, per, _ = q.shape
    rank = upv.shape[0]
    rows = ndevs * per
    positions = cache.shape[1]
    where = jnp.stack([mine, jnp.full_like(mine, ndevs)]).astype(jnp.int32)
    whole = lambda a: pl.BlockSpec(a.shape, lambda i, *_: (0,) * a.ndim)
    return pl.pallas_call(
        functools.partial(flash_kernel, hl),
        out_shape=(
            jax.ShapeDtypeStruct((ndevs, R, per, HD), BF),
            jax.ShapeDtypeStruct((R, rows, 128), F32),
        ),
        grid_spec=pltpu.PrefetchScalarGridSpec(
            num_scalar_prefetch=2,
            grid=(R,),
            in_specs=[
                whole(q),
                pl.BlockSpec((1,) + fresh.shape[1:], lambda i, *_: (i, 0, 0)),
                pl.BlockSpec((1, positions, 2 * rank), lambda i, *_: (i, 0, 0)),
                whole(upk),
                whole(upv),
            ],
            out_specs=[
                pl.BlockSpec((ndevs, R, per, HD), lambda i, *_: (0, 0, 0, 0)),
                pl.BlockSpec((1, rows, 128), lambda i, *_: (i, 0, 0)),
            ],
            scratch_shapes=[
                pltpu.VMEM((ndevs, R, per, rank), BF),
                pltpu.VMEM((ndevs, R, per, rank), BF),
                pltpu.VMEM((ndevs, R, per, rank), BF),
            ],
        ),
        compiler_params=pltpu.CompilerParams(vmem_limit_bytes=56 * 2 ** 20),
        cost_estimate=pl.CostEstimate(
            flops=2 * R * rows * positions * rank * 3,
            bytes_accessed=cache.size * 2,
            transcendentals=R * rows * positions,
        ),
        name="flash",
    )(lengths, where, q, fresh, cache, upk, upv)


def local(hidden_in, latent_cache, lengths, placement, w_query, w_down, up_key, up_value, w_out):
    ndevs = lax.axis_size("xfer")
    mine = lax.axis_index("xfer")
    rank = up_key.shape[0]
    width = hidden_in.shape[2]
    hl = w_query.shape[1] // HD
    slot_rows = hidden_in.shape[0]
    samples = slot_rows * ndevs // R
    nrows = slot_rows * 2 * ndevs
    per = samples * 2 * hl
    x = lax.all_gather(hidden_in.reshape(slot_rows * 2, width), "xfer", axis=0, tiled=True)
    query = jnp.dot(x, w_query, preferred_element_type=F32).astype(BF)
    fresh = jnp.dot(x, w_down, preferred_element_type=F32).astype(BF)
    q = lax.all_gather(query.reshape(R, per, HD), "xfer", axis=0)
    own = lax.all_gather(fresh, "xfer", axis=1, tiled=True)
    own = own.reshape(R, samples * 2, 2 * rank)
    pad = -(samples * 2) % 16
    own = jnp.pad(own, ((0, 0), (0, pad), (0, 0)))
    o, lse = flash(q, own, latent_cache, lengths, up_key.T, up_value, mine, ndevs, hl)
    lse = lse[:, :, 0].reshape(R, ndevs, per).transpose(1, 0, 2)
    o = lax.all_to_all(o, "xfer", split_axis=0, concat_axis=0, tiled=True)
    lse = lax.all_to_all(lse, "xfer", split_axis=0, concat_axis=0, tiled=True)
    share = jax.nn.softmax(lse, axis=0)
    head_out = jnp.sum(o.astype(F32) * share[..., None], axis=0).astype(BF)
    head_out = head_out.reshape(R, samples * 2, hl * HD)[placement].reshape(nrows, hl * HD)
    part = jnp.dot(head_out, w_out, preferred_element_type=F32).astype(BF)
    part = lax.all_to_all(
        part.reshape(ndevs, slot_rows * 2, width), "xfer", split_axis=0, concat_axis=0, tiled=True
    )
    summed = jnp.sum(part.astype(F32), axis=0).astype(BF)
    return summed.reshape(slot_rows, 2, width)


def solution(mesh):
    placed = (
        P(("parts", "xfer"), None, None),
        P("parts", "xfer", None),
        P("parts"),
        P("parts"),
        P(None, "xfer"),
        P(None, "xfer"),
        P(),
        P(),
        P("xfer", None),
    )
    return jax.shard_map(
        local,
        mesh=mesh,
        in_specs=placed,
        out_specs=P(("parts", "xfer"), None, None),
        check_vma=False,
    )
```

```python
import functools

import jax
import jax.numpy as jnp
from jax import lax
from jax.experimental import pallas as pl
from jax.experimental.pallas import tpu as pltpu
from jax.sharding import PartitionSpec as P

HEADS = 64
KVH = 8
HD = 128
R = 16
NEG = -1e30
BF = jnp.bfloat16
F32 = jnp.float32


def dot_nt(a, b):
    return lax.dot_general(a, b, (((1,), (1,)), ((), ())), preferred_element_type=F32)


def flash_kernel(hl, lengths_ref, where_ref, q_ref, fresh_ref, cache_ref, upk_ref, upv_ref,
                 o_ref, lse_ref, hi_ref, lo_ref, lat_ref):
    ndevs, _, per, _ = q_ref.shape
    rank = upk_ref.shape[1]
    rows = ndevs * per
    each = ndevs // KVH
    positions = cache_ref.shape[1]
    req = pl.program_id(0)

    @pl.when(req == 0)
    def _():
        for g in range(KVH):
            qg = q_ref[g * each:(g + 1) * each].reshape(each * R * per, HD)
            a = jnp.dot(qg, upk_ref[g * HD:(g + 1) * HD], preferred_element_type=F32)
            a = a * (HD ** -0.5)
            hi = a.astype(BF)
            lo = (a - hi.astype(F32)).astype(BF)
            hi_ref[g * each:(g + 1) * each] = hi.reshape(each, R, per, rank)
            lo_ref[g * each:(g + 1) * each] = lo.reshape(each, R, per, rank)

    first = where_ref[0] * positions
    seen = lengths_ref[req] - first
    last = where_ref[0] == where_ref[1] - 1

    qh = hi_ref[:, pl.ds(req, 1)].reshape(rows, rank)
    ql = lo_ref[:, pl.ds(req, 1)].reshape(rows, rank)
    key = cache_ref[0, :, :rank]
    val = cache_ref[0, :, rank:]
    s = dot_nt(qh, key) + dot_nt(ql, key)
    pos = lax.broadcasted_iota(jnp.int32, s.shape, 1)
    s = jnp.where(pos < seen, s, NEG)
    fk = fresh_ref[0, :, :rank]
    fv = fresh_ref[0, :, rank:]
    n = dot_nt(qh, fk) + dot_nt(ql, fk)
    row = lax.broadcasted_iota(jnp.int32, n.shape, 0) % per
    col = lax.broadcasted_iota(jnp.int32, n.shape, 1)
    rs, rt = row // (2 * hl), (row // hl) % 2
    ok = (rs == col // 2) & (col % 2 <= rt) & last
    n = jnp.where(ok, n, NEG)
    top = jnp.maximum(jnp.max(s, axis=1, keepdims=True), jnp.max(n, axis=1, keepdims=True))
    p = jnp.exp(s - top)
    pn = jnp.exp(n - top)
    total = jnp.sum(p, axis=1, keepdims=True) + jnp.sum(pn, axis=1, keepdims=True)
    acc = jnp.dot(p.astype(BF), val, preferred_element_type=F32)
    acc = acc + jnp.dot(pn.astype(BF), fv, preferred_element_type=F32)
    lat_ref[:, pl.ds(req, 1)] = (acc / total).astype(BF).reshape(ndevs, 1, per, rank)
    lse_ref[0] = jnp.broadcast_to(top + jnp.log(total), (rows, 128))

    @pl.when(req == R - 1)
    def _():
        for g in range(KVH):
            lg = lat_ref[g * each:(g + 1) * each].reshape(each * R * per, rank)
            o = jnp.dot(lg, upv_ref[:, g * HD:(g + 1) * HD], preferred_element_type=F32)
            o_ref[g * each:(g + 1) * each] = o.astype(BF).reshape(each, R, per, HD)


def flash(q, fresh, cache, lengths, upk, upv, mine, ndevs, hl):
    _, _, per, _ = q.shape
    rank = upv.shape[0]
    rows = ndevs * per
    positions = cache.shape[1]
    where = jnp.stack([mine, jnp.full_like(mine, ndevs)]).astype(jnp.int32)
    whole = lambda a: pl.BlockSpec(a.shape, lambda i, *_: (0,) * a.ndim)
    return pl.pallas_call(
        functools.partial(flash_kernel, hl),
        out_shape=(
            jax.ShapeDtypeStruct((ndevs, R, per, HD), BF),
            jax.ShapeDtypeStruct((R, rows, 128), F32),
        ),
        grid_spec=pltpu.PrefetchScalarGridSpec(
            num_scalar_prefetch=2,
            grid=(R,),
            in_specs=[
                whole(q),
                pl.BlockSpec((1,) + fresh.shape[1:], lambda i, *_: (i, 0, 0)),
                pl.BlockSpec((1, positions, 2 * rank), lambda i, *_: (i, 0, 0)),
                whole(upk),
                whole(upv),
            ],
            out_specs=[
                pl.BlockSpec((ndevs, R, per, HD), lambda i, *_: (0, 0, 0, 0)),
                pl.BlockSpec((1, rows, 128), lambda i, *_: (i, 0, 0)),
            ],
            scratch_shapes=[
                pltpu.VMEM((ndevs, R, per, rank), BF),
                pltpu.VMEM((ndevs, R, per, rank), BF),
                pltpu.VMEM((ndevs, R, per, rank), BF),
            ],
        ),
        compiler_params=pltpu.CompilerParams(vmem_limit_bytes=56 * 2 ** 20),
        cost_estimate=pl.CostEstimate(
            flops=2 * R * rows * positions * rank * 3,
            bytes_accessed=cache.size * 2,
            transcendentals=R * rows * positions,
        ),
        name="flash",
    )(lengths, where, q, fresh, cache, upk, upv)


def place(ndevs):
    me = lax.axis_index("xfer")
    return me // 4, (me // 2) % 2, me % 2


def index_of(z, y, c):
    return z * 4 + y * 2 + c


def greet(ndevs):
    deep = ndevs // 4
    z, y, c = place(ndevs)
    barrier = pltpu.get_barrier_semaphore()
    peers = [index_of((z + k) % deep, y, c) for k in range(1, deep)]
    peers += [index_of(z, 1 - y, c), index_of(z, y, 1 - c)]
    for peer in peers:
        pl.semaphore_signal(barrier, inc=1, device_id={"xfer": peer}, device_id_type=pl.DeviceIdType.MESH)
    pl.semaphore_wait(barrier, len(peers))


def remote(src, dst, send, recv, peer):
    return pltpu.make_async_remote_copy(
        src_ref=src, dst_ref=dst, send_sem=send, recv_sem=recv,
        device_id={"xfer": peer}, device_id_type=pl.DeviceIdType.MESH,
    )


def spread(ndevs, buf, send, recv):
    deep = ndevs // 4
    z, y, c = place(ndevs)
    far, near, twin = 0, deep, 2 * deep

    def move(block, slot, peer):
        return remote(buf.at[block], buf.at[block], send.at[slot], recv.at[slot], peer)

    mine = index_of(z, y, c)
    along = [move(mine, far + k, index_of((z + k) % deep, y, c)) for k in range(1, deep)]
    for copy in along:
        copy.start()
    across, over = [], []
    for k in range(deep + 1):
        if k < deep:
            block = index_of((z - k + deep) % deep, y, c)
            if k:
                along[k - 1].wait_recv()
            across.append(move(block, near + k, index_of(z, 1 - y, c)))
            across[-1].start()
            over.append(move(block, twin + k, index_of(z, y, 1 - c)))
            over[-1].start()
        if k:
            across[k - 1].wait_recv()
            block = index_of((z - k + 1 + deep) % deep, 1 - y, c)
            over.append(move(block, twin + deep + k - 1, index_of(z, y, 1 - c)))
            over[-1].start()
    for copy in over:
        copy.wait_recv()
    for copy in along + across + over:
        copy.wait_send()


def project_kernel(ndevs, hidden_ref, wq_ref, wd_ref, out_ref,
                   x_ref, wide_ref, wqv_ref, wdv_ref, stage_ref, send, recv, send2, recv2, wsem):
    copies = [
        pltpu.make_async_copy(wq_ref, wqv_ref, wsem.at[0]),
        pltpu.make_async_copy(wd_ref, wdv_ref, wsem.at[1]),
    ]
    for copy in copies:
        copy.start()
    me = lax.axis_index("xfer")
    slots, _, width = hidden_ref.shape
    tiles = width // HD
    nrows = ndevs * slots * 2
    hl = wqv_ref.shape[1] // HD
    fw = wdv_ref.shape[1]
    for s in range(slots):
        for t in range(tiles):
            wide_ref[pl.ds(s * 2 * tiles + t, 2, stride=tiles), :] = (
                hidden_ref[s, :, t * HD:(t + 1) * HD].astype(F32))
    x_ref[pl.ds(me, 1)] = wide_ref[:slots * 2 * tiles, :].astype(BF)[None]
    greet(ndevs)
    spread(ndevs, x_ref, send, recv)
    wide_ref[...] = x_ref[...].astype(F32).reshape(wide_ref.shape)
    for copy in copies:
        copy.wait()
    query = jnp.zeros((nrows, hl * HD), F32)
    fresh = jnp.zeros((nrows, fw), F32)
    step = 16
    for t in range(0, tiles, step):
        xt = jnp.concatenate(
            [wide_ref[pl.ds(t + i, nrows, stride=tiles), :].astype(BF) for i in range(step)], axis=1)
        span = slice(t * HD, (t + step) * HD)
        query = query + jnp.dot(xt, wqv_ref[span], preferred_element_type=F32)
        fresh = fresh + jnp.dot(xt, wdv_ref[span], preferred_element_type=F32)
    for h in range(hl):
        stage_ref[pl.ds(h, nrows, stride=hl), :] = query[:, h * HD:(h + 1) * HD]
    stage_ref[nrows * hl:, :] = jnp.zeros((nrows, HD), F32)
    stage_ref[nrows * hl:, :fw] = fresh
    out_ref[pl.ds(me, 1)] = stage_ref[...].astype(BF)[None]
    spread(ndevs, out_ref, send2, recv2)


def project(hidden, wq, wd, ndevs):
    slots, _, width = hidden.shape
    tall = slots * 2 * width // HD
    nrows = ndevs * slots * 2
    hl = wq.shape[1] // HD
    sems = pltpu.SemaphoreType.DMA((ndevs,))
    return pl.pallas_call(
        functools.partial(project_kernel, ndevs),
        out_shape=jax.ShapeDtypeStruct((ndevs, nrows * (hl + 1), HD), BF),
        in_specs=[
            pl.BlockSpec(memory_space=pltpu.VMEM),
            pl.BlockSpec(memory_space=pl.ANY),
            pl.BlockSpec(memory_space=pl.ANY),
        ],
        out_specs=pl.BlockSpec(memory_space=pltpu.VMEM),
        scratch_shapes=[
            pltpu.VMEM((ndevs, tall, HD), BF),
            pltpu.VMEM((ndevs * tall, HD), F32),
            pltpu.VMEM(wq.shape, BF),
            pltpu.VMEM(wd.shape, BF),
            pltpu.VMEM((nrows * (hl + 1), HD), F32),
            sems, sems, sems, sems,
            pltpu.SemaphoreType.DMA((2,)),
        ],
        compiler_params=pltpu.CompilerParams(
            collective_id=0, has_side_effects=True, vmem_limit_bytes=56 * 2 ** 20),
        name="project",
    )(hidden, wq, wd)


def fold(ndevs, blocks, held1, held2, held3, send, recv, merge, finish):
    deep = ndevs // 4
    z, y, c = place(ndevs)
    many = len(blocks)
    at = lambda refs, i: [r.at[i] for r in refs]
    count = [0]

    def ship(src, dst, peer):
        copies = []
        for s, d in zip(src, dst):
            copies.append(remote(s, d, send.at[count[0]], recv.at[count[0]], peer))
            count[0] += 1
        for copy in copies:
            copy.start()
        return copies

    def arrive(copies):
        for copy in copies:
            copy.wait_recv()

    order = [(z + k) % deep for k in range(1, deep + 1)]
    twin = index_of(z, y, 1 - c)
    first = []
    for far in (1, 0):
        yy = 1 - y if far else y
        for k in range(deep):
            first.append(ship(at(blocks, index_of(order[k], yy, 1 - c)), at(held1, far * deep + k), twin))
    second = []
    for k in range(deep):
        arrive(first[k])
        here = at(blocks, index_of(order[k], 1 - y, c))
        merge(here, here, at(held1, deep + k))
        second.append(ship(here, at(held2, k), index_of(z, 1 - y, c)))
    for k in range(deep):
        arrive(first[deep + k])
        here = at(blocks, index_of(order[k], y, c))
        merge(here, here, at(held1, k))
    third = []
    for k in range(deep):
        arrive(second[k])
        here = at(blocks, index_of(order[k], y, c))
        merge(here, here, at(held2, k))
        if k < deep - 1:
            third.append(ship(here, at(held3, k), index_of(order[k], y, c)))
    for copies in third:
        arrive(copies)
    finish(at(blocks, index_of(z, y, c)), [at(held3, k) for k in range(deep - 1)])
    for copies in first + second + third:
        for copy in copies:
            copy.wait_send()


def turn(w):
    return jnp.transpose(jnp.broadcast_to(w, (HD, HD)))


def merge_heads(dst, a, b):
    n = a[0].shape[0] // HD
    la, lb = a[1][...], b[1][...]
    top = jnp.maximum(la, lb)
    ea, eb = jnp.exp(la - top), jnp.exp(lb - top)
    both = ea + eb
    share = ea / both
    lse = top + jnp.log(both)
    for t in range(n):
        span = slice(t * HD, (t + 1) * HD)
        oa, ob = a[0][span].astype(F32), b[0][span].astype(F32)
        dst[0][span] = (ob + turn(share[t:t + 1]) * (oa - ob)).astype(BF)
    dst[1][...] = lse


def merge_sums(dst, a, b):
    dst[0][...] = (a[0][...].astype(F32) + b[0][...].astype(F32)).astype(BF)


def finish_kernel(ndevs, o_ref, l_ref, perm_ref, wo_ref, out_ref,
                  ob_ref, lb_ref, o1, l1, o2, l2, o3, l3, wov_ref, head_ref, wide_ref, *rest):
    pieces = (len(rest) - 3) // 4
    sums = rest[:4 * pieces]
    send, recv, wsem = rest[-3:]
    copies = [
        pltpu.make_async_copy(wo_ref, wov_ref, wsem.at[0]),
    ]
    for copy in copies:
        copy.start()
    deep = ndevs // 4
    slots, _, width = out_ref.shape
    nrows = ndevs * slots * 2
    hl = wov_ref.shape[0] // HD
    tiles = width // HD // pieces
    ob_ref[...] = o_ref[...]
    lb_ref[...] = l_ref[...]
    greet(ndevs)

    def finish_heads(mine, others):
        n = mine[0].shape[0] // HD
        ls = [mine[1][...]] + [o[1][...] for o in others]
        top = functools.reduce(jnp.maximum, ls)
        es = [jnp.exp(l - top) for l in ls]
        both = functools.reduce(jnp.add, es)
        for t in range(n):
            span = slice(t * HD, (t + 1) * HD)
            got = jnp.zeros((HD, HD), F32)
            for e, o in zip(es, [mine] + list(others)):
                got = got + turn((e / both)[t:t + 1]) * o[0][span].astype(F32)
            head_ref[span] = got

    fold(ndevs, (ob_ref, lb_ref), (o1, l1), (o2, l2), (o3, l3),
         send.at[0], recv.at[0], merge_heads, finish_heads)
    heads = [head_ref[pl.ds(h, nrows, stride=hl), :].astype(BF) for h in range(hl)]
    head = jnp.concatenate(heads, axis=1)
    head = jnp.dot(perm_ref[...], head, preferred_element_type=F32).astype(BF)
    for copy in copies:
        copy.wait()
    for p in range(pieces):
        step = 8
        for t in range(0, tiles, step):
            at = (p * tiles + t) * HD
            got = jnp.dot(head, wov_ref[:, at:at + step * HD], preferred_element_type=F32)
            for i in range(step):
                wide_ref[pl.ds(t + i, nrows, stride=tiles), :] = got[:, i * HD:(i + 1) * HD]
        buf = sums[4 * p]
        buf[...] = wide_ref[...].astype(BF).reshape(buf.shape)

        def finish_sums(mine, others, p=p):
            total = mine[0][...].astype(F32)
            for o in others:
                total = total + o[0][...].astype(F32)
            wide_ref[:slots * 2 * tiles, :] = total
            for s in range(slots):
                for t in range(tiles):
                    at = (p * tiles + t) * HD
                    out_ref[s, :, at:at + HD] = (
                        wide_ref[pl.ds(s * 2 * tiles + t, 2, stride=tiles), :].astype(BF))

        fold(ndevs, (buf,), (sums[4 * p + 1],), (sums[4 * p + 2],), (sums[4 * p + 3],),
             send.at[1 + p], recv.at[1 + p], merge_sums, finish_sums)


def finish(o, lse, perm, wo, ndevs, slots, pieces=1):
    width = wo.shape[1]
    deep = ndevs // 4
    rows = o.shape[1]
    nrows = ndevs * slots * 2
    tall = slots * 2 * width // HD // pieces
    sizes = (ndevs, 2 * deep, deep, deep - 1)
    scratch = [pltpu.VMEM(o.shape, BF), pltpu.VMEM(lse.shape, F32)]
    for n in sizes[1:]:
        scratch += [pltpu.VMEM((n, rows, HD), BF), pltpu.VMEM((n,) + lse.shape[1:], F32)]
    scratch += [
        pltpu.VMEM(wo.shape, BF),
        pltpu.VMEM((rows, HD), F32),
        pltpu.VMEM((ndevs * tall, HD), F32),
    ]
    for _ in range(pieces):
        scratch += [pltpu.VMEM((n, tall, HD), BF) for n in sizes]
    sems = pltpu.SemaphoreType.DMA((1 + pieces, 8 * deep))
    scratch += [sems, sems, pltpu.SemaphoreType.DMA((1,))]
    return pl.pallas_call(
        functools.partial(finish_kernel, ndevs),
        out_shape=jax.ShapeDtypeStruct((slots, 2, width), BF),
        in_specs=[pl.BlockSpec(memory_space=pltpu.VMEM)] * 3 + [pl.BlockSpec(memory_space=pl.ANY)],
        out_specs=pl.BlockSpec(memory_space=pltpu.VMEM),
        scratch_shapes=scratch,
        compiler_params=pltpu.CompilerParams(
            collective_id=1, has_side_effects=True, vmem_limit_bytes=56 * 2 ** 20),
        name="finish",
    )(o, lse, perm, wo)


def local(hidden_in, latent_cache, lengths, placement, w_query, w_down, up_key, up_value, w_out):
    ndevs = lax.axis_size("xfer")
    mine = lax.axis_index("xfer")
    rank = up_key.shape[0]
    hl = w_query.shape[1] // HD
    fw = w_down.shape[1]
    slot_rows = hidden_in.shape[0]
    samples = slot_rows * ndevs // R
    nrows = slot_rows * 2 * ndevs
    per = samples * 2 * hl
    both = project(hidden_in, w_query, w_down, ndevs)
    q = both[:, :nrows * hl].reshape(ndevs, R, per, HD)
    own = both[:, nrows * hl:, :fw].transpose(1, 0, 2).reshape(R, samples * 2, 2 * rank)
    pad = -(samples * 2) % 16
    own = jnp.pad(own, ((0, 0), (0, pad), (0, 0)))
    o, lse = flash(q, own, latent_cache, lengths, up_key.T, up_value, mine, ndevs, hl)
    lse = lse[:, :, 0].reshape(R, ndevs, per).transpose(1, 0, 2).reshape(ndevs, R * per // HD, HD)
    lse = jnp.pad(lse, ((0, 0), (0, 8 - R * per // HD), (0, 0)))
    slot = jnp.arange(nrows, dtype=jnp.int32)
    source = jnp.repeat(placement, 2 * samples) * (2 * samples) + slot % (2 * samples)
    perm = (source[:, None] == slot[None, :]).astype(BF)
    return finish(o.reshape(ndevs, R * per, HD), lse, perm, w_out, ndevs, slot_rows)


def solution(mesh):
    placed = (
        P(("parts", "xfer"), None, None),
        P("parts", "xfer", None),
        P("parts"),
        P("parts"),
        P(None, "xfer"),
        P(None, "xfer"),
        P(),
        P(),
        P("xfer", None),
    )
    return jax.shard_map(
        local,
        mesh=mesh,
        in_specs=placed,
        out_specs=P(("parts", "xfer"), None, None),
        check_vma=False,
    )
```

```python
import functools

import jax
import jax.numpy as jnp
from jax import lax
from jax.experimental import pallas as pl
from jax.experimental.pallas import tpu as pltpu
from jax.sharding import PartitionSpec as P

HEADS = 64
KVH = 8
HD = 128
R = 16
NEG = -1e30
LOG2E = 1.4426950408889634
BF = jnp.bfloat16
F32 = jnp.float32


def dot_nt(a, b):
    return lax.dot_general(a, b, (((1,), (1,)), ((), ())), preferred_element_type=F32)


def flash_kernel(hl, lengths_ref, both_ref, fresh_ref, cache_ref, upk_ref, upv_ref,
                 o_ref, lse_ref, hi_ref, lo_ref, lat_ref):
    ndevs = both_ref.shape[0]
    _, _, per, rank = hi_ref.shape
    rows = ndevs * per
    each = ndevs // KVH
    batch, positions, _ = cache_ref.shape
    step = pl.program_id(0)
    me = lax.axis_index("xfer")

    @pl.when(step == 0)
    def _():
        for g in range(KVH):
            qg = both_ref[g * each:(g + 1) * each, :R * per].reshape(each * R * per, HD)
            a = dot_nt(qg, upk_ref[:, g * HD:(g + 1) * HD])
            a = a * (HD ** -0.5 * LOG2E)
            hi = a.astype(BF)
            lo = (a - hi.astype(F32)).astype(BF)
            hi_ref[g * each:(g + 1) * each] = hi.reshape(each, R, per, rank)
            lo_ref[g * each:(g + 1) * each] = lo.reshape(each, R, per, rank)
        lse_ref[...] = jnp.zeros_like(lse_ref)

    lane = lax.broadcasted_iota(jnp.int32, (rows, HD), 1)

    def scores(req, keys):
        qh = hi_ref[:, pl.ds(req, 1)].reshape(rows, rank)
        ql = lo_ref[:, pl.ds(req, 1)].reshape(rows, rank)
        return dot_nt(qh, keys) + dot_nt(ql, keys)

    def weigh(s, vals):
        top = jnp.max(s, axis=1, keepdims=True)
        p = jnp.exp2(s - top)
        total = jnp.sum(p, axis=1, keepdims=True)
        acc = jnp.dot(p.astype(BF), vals, preferred_element_type=F32)
        return acc / total, top + jnp.log2(total)

    pos = lax.broadcasted_iota(jnp.int32, (rows, positions), 1)
    lses = lse_ref[...].reshape(rows, HD)
    ahead = scores(step * batch, cache_ref[0, :, :rank])
    for b in range(batch):
        req = step * batch + b
        s = ahead
        if b + 1 < batch:
            ahead = scores(req + 1, cache_ref[b + 1, :, :rank])
        s = jnp.where(pos < lengths_ref[req] - me * positions, s, NEG)
        out, lse = weigh(s, cache_ref[b, :, rank:])
        lat_ref[:, pl.ds(req, 1)] = out.astype(BF).reshape(ndevs, 1, per, rank)
        lses = jnp.where(lane == req, lse, lses)
    lse_ref[...] = lses.reshape(lse_ref.shape)

    @pl.when(me // batch == step)
    def _():
        n = scores(me, fresh_ref[:, :rank])
        row = lax.broadcasted_iota(jnp.int32, n.shape, 0) % per
        col = lax.broadcasted_iota(jnp.int32, n.shape, 1)
        rs, rt = row // (2 * hl), (row // hl) % 2
        n = jnp.where((rs == col // 2) & (col % 2 <= rt), n, NEG)
        near, near_lse = weigh(n, fresh_ref[:, rank:])
        lses = lse_ref[...].reshape(rows, HD)
        far_lse = jnp.sum(jnp.where(lane == me, lses, 0.0), axis=1, keepdims=True)
        far = lat_ref[:, pl.ds(me, 1)].reshape(rows, rank).astype(F32)
        top = jnp.maximum(near_lse, far_lse)
        en, ef = jnp.exp2(near_lse - top), jnp.exp2(far_lse - top)
        out = far + (en / (en + ef)) * (near - far)
        lat_ref[:, pl.ds(me, 1)] = out.astype(BF).reshape(ndevs, 1, per, rank)
        lse = top + jnp.log2(en + ef)
        lse_ref[...] = jnp.where(lane == me, lse, lses).reshape(lse_ref.shape)

    @pl.when(step == R // batch - 1)
    def _():
        for g in range(KVH):
            lg = lat_ref[g * each:(g + 1) * each].reshape(each * R * per, rank)
            o = jnp.dot(lg, upv_ref[:, g * HD:(g + 1) * HD], preferred_element_type=F32)
            o_ref[g * each:(g + 1) * each] = o.astype(BF).reshape(each, R * per, HD)


def flash(both, fresh, cache, lengths, upk, upv, hl, per, batch=4):
    ndevs = both.shape[0]
    rank = upv.shape[0]
    rows = ndevs * per
    positions = cache.shape[1]
    whole = lambda shape: pl.BlockSpec(shape, lambda i, *_: (0,) * len(shape))
    state = pltpu.VMEM((ndevs, R, per, rank), BF)
    return pl.pallas_call(
        functools.partial(flash_kernel, hl),
        out_shape=(
            jax.ShapeDtypeStruct((ndevs, R * per, HD), BF),
            jax.ShapeDtypeStruct((ndevs, per, HD), F32),
        ),
        grid_spec=pltpu.PrefetchScalarGridSpec(
            num_scalar_prefetch=1,
            grid=(R // batch,),
            in_specs=[
                whole(both.shape),
                whole(fresh.shape),
                pl.BlockSpec((batch, positions, 2 * rank), lambda i, *_: (i, 0, 0)),
                whole(upk.shape),
                whole(upv.shape),
            ],
            out_specs=[whole((ndevs, R * per, HD)), whole((ndevs, per, HD))],
            scratch_shapes=[state, state, state],
        ),
        compiler_params=pltpu.CompilerParams(vmem_limit_bytes=60 * 2 ** 20),
        cost_estimate=pl.CostEstimate(
            flops=2 * R * rows * positions * rank * 3,
            bytes_accessed=cache.size * 2,
            transcendentals=R * rows * positions,
        ),
        name="flash",
    )(lengths, both, fresh, cache, upk, upv)


def place(ndevs):
    me = lax.axis_index("xfer")
    return me // 4, (me // 2) % 2, me % 2


def index_of(z, y, c):
    return z * 4 + y * 2 + c


def greet(ndevs):
    deep = ndevs // 4
    z, y, c = place(ndevs)
    barrier = pltpu.get_barrier_semaphore()
    peers = [index_of((z + k) % deep, y, c) for k in range(1, deep)]
    peers += [index_of(z, 1 - y, c), index_of(z, y, 1 - c)]
    for peer in peers:
        pl.semaphore_signal(barrier, inc=1, device_id={"xfer": peer}, device_id_type=pl.DeviceIdType.MESH)
    pl.semaphore_wait(barrier, len(peers))


def remote(src, dst, send, recv, peer):
    return pltpu.make_async_remote_copy(
        src_ref=src, dst_ref=dst, send_sem=send, recv_sem=recv,
        device_id={"xfer": peer}, device_id_type=pl.DeviceIdType.MESH,
    )


def spread(ndevs, buf, send, recv):
    deep = ndevs // 4
    z, y, c = place(ndevs)
    far, near, twin = 0, deep, 2 * deep

    def move(block, slot, peer):
        return remote(buf.at[block], buf.at[block], send.at[slot], recv.at[slot], peer)

    mine = index_of(z, y, c)
    along = [move(mine, far + k, index_of((z + k) % deep, y, c)) for k in range(1, deep)]
    for copy in along:
        copy.start()
    across, over = [], []
    for k in range(deep + 1):
        if k < deep:
            block = index_of((z - k + deep) % deep, y, c)
            if k:
                along[k - 1].wait_recv()
            across.append(move(block, near + k, index_of(z, 1 - y, c)))
            across[-1].start()
            over.append(move(block, twin + k, index_of(z, y, 1 - c)))
            over[-1].start()
        if k:
            across[k - 1].wait_recv()
            block = index_of((z - k + 1 + deep) % deep, 1 - y, c)
            over.append(move(block, twin + deep + k - 1, index_of(z, y, 1 - c)))
            over[-1].start()
    for copy in over:
        copy.wait_recv()
    for copy in along + across + over:
        copy.wait_send()


def project_kernel(ndevs, hidden_ref, wq_ref, wd_ref, out_ref,
                   x_ref, wide_ref, wqv_ref, wdv_ref, stage_ref, send, recv, send2, recv2, wsem):
    copies = [
        pltpu.make_async_copy(wq_ref, wqv_ref, wsem.at[0]),
        pltpu.make_async_copy(wd_ref, wdv_ref, wsem.at[1]),
    ]
    for copy in copies:
        copy.start()
    me = lax.axis_index("xfer")
    slots, _, width = hidden_ref.shape
    tiles = width // HD
    nrows = ndevs * slots * 2
    hl = wqv_ref.shape[1] // HD
    fw = wdv_ref.shape[0]
    for s in range(slots):
        for t in range(tiles):
            wide_ref[pl.ds(s * 2 * tiles + t, 2, stride=tiles), :] = (
                hidden_ref[s, :, t * HD:(t + 1) * HD].astype(F32))
    x_ref[pl.ds(me, 1)] = wide_ref[:slots * 2 * tiles, :].astype(BF)[None]
    greet(ndevs)
    spread(ndevs, x_ref, send, recv)
    wide_ref[...] = x_ref[...].astype(F32).reshape(wide_ref.shape)
    for copy in copies:
        copy.wait()
    query = jnp.zeros((nrows, hl * HD), F32)
    fresh = jnp.zeros((nrows, fw), F32)
    step = 16
    for t in range(0, tiles, step):
        xt = jnp.concatenate(
            [wide_ref[pl.ds(t + i, nrows, stride=tiles), :].astype(BF) for i in range(step)], axis=1)
        span = slice(t * HD, (t + step) * HD)
        query = query + jnp.dot(xt, wqv_ref[span], preferred_element_type=F32)
        fresh = fresh + dot_nt(xt, wdv_ref[:, span])
    for h in range(hl):
        stage_ref[pl.ds(h, nrows, stride=hl), :] = query[:, h * HD:(h + 1) * HD]
    stage_ref[nrows * hl:, :] = jnp.zeros((nrows, HD), F32)
    stage_ref[nrows * hl:, :fw] = fresh
    out_ref[pl.ds(me, 1)] = stage_ref[...].astype(BF)[None]
    spread(ndevs, out_ref, send2, recv2)


def project(hidden, wq, wd, ndevs):
    slots, _, width = hidden.shape
    tall = slots * 2 * width // HD
    nrows = ndevs * slots * 2
    hl = wq.shape[1] // HD
    sems = pltpu.SemaphoreType.DMA((ndevs,))
    return pl.pallas_call(
        functools.partial(project_kernel, ndevs),
        out_shape=jax.ShapeDtypeStruct((ndevs, nrows * (hl + 1), HD), BF),
        in_specs=[
            pl.BlockSpec(memory_space=pltpu.VMEM),
            pl.BlockSpec(memory_space=pl.ANY),
            pl.BlockSpec(memory_space=pl.ANY),
        ],
        out_specs=pl.BlockSpec(memory_space=pltpu.VMEM),
        scratch_shapes=[
            pltpu.VMEM((ndevs, tall, HD), BF),
            pltpu.VMEM((ndevs * tall, HD), F32),
            pltpu.VMEM(wq.shape, BF),
            pltpu.VMEM(wd.shape, BF),
            pltpu.VMEM((nrows * (hl + 1), HD), F32),
            sems, sems, sems, sems,
            pltpu.SemaphoreType.DMA((2,)),
        ],
        compiler_params=pltpu.CompilerParams(
            collective_id=0, has_side_effects=True, vmem_limit_bytes=56 * 2 ** 20),
        name="project",
    )(hidden, wq, wd)


def fold(ndevs, blocks, held1, held2, held3, send, recv, merge, finish):
    deep = ndevs // 4
    z, y, c = place(ndevs)
    many = len(blocks)
    at = lambda refs, i: [r.at[i] for r in refs]
    count = [0]

    def ship(src, dst, peer):
        copies = []
        for s, d in zip(src, dst):
            copies.append(remote(s, d, send.at[count[0]], recv.at[count[0]], peer))
            count[0] += 1
        for copy in copies:
            copy.start()
        return copies

    def arrive(copies):
        for copy in copies:
            copy.wait_recv()

    order = [(z + k) % deep for k in range(1, deep + 1)]
    twin = index_of(z, y, 1 - c)
    first = []
    for far in (1, 0):
        yy = 1 - y if far else y
        for k in range(deep):
            first.append(ship(at(blocks, index_of(order[k], yy, 1 - c)), at(held1, far * deep + k), twin))
    second = []
    for k in range(deep):
        arrive(first[k])
        here = at(blocks, index_of(order[k], 1 - y, c))
        merge(here, here, at(held1, deep + k))
        second.append(ship(here, at(held2, k), index_of(z, 1 - y, c)))
    for k in range(deep):
        arrive(first[deep + k])
        here = at(blocks, index_of(order[k], y, c))
        merge(here, here, at(held1, k))
    third = []
    for k in range(deep):
        arrive(second[k])
        here = at(blocks, index_of(order[k], y, c))
        merge(here, here, at(held2, k))
        if k < deep - 1:
            third.append(ship(here, at(held3, k), index_of(order[k], y, c)))
    for copies in third:
        arrive(copies)
    finish(at(blocks, index_of(z, y, c)), [at(held3, k) for k in range(deep - 1)])
    for copies in first + second + third:
        for copy in copies:
            copy.wait_send()


def weighted(terms):
    per = terms[0][0].shape[0]
    for req in range(R):
        span = slice(req * per, (req + 1) * per)
        got = None
        for share, block in terms:
            term = share[:, req:req + 1] * block[span].astype(F32)
            got = term if got is None else got + term
        yield span, got


def merge_heads(dst, a, b):
    la, lb = a[1][...], b[1][...]
    top = jnp.maximum(la, lb)
    ea, eb = jnp.exp2(la - top), jnp.exp2(lb - top)
    both = ea + eb
    for span, got in weighted([(ea / both, a[0]), (eb / both, b[0])]):
        dst[0][span] = got.astype(BF)
    dst[1][...] = top + jnp.log2(both)


def merge_sums(dst, a, b):
    dst[0][...] = (a[0][...].astype(F32) + b[0][...].astype(F32)).astype(BF)


def finish_kernel(ndevs, o_ref, l_ref, place_ref, wo_ref, out_ref,
                  ob_ref, lb_ref, o1, l1, o2, l2, o3, l3, wov_ref, head_ref, wide_ref, *rest):
    pieces = (len(rest) - 3) // 4
    sums = rest[:4 * pieces]
    send, recv, wsem = rest[-3:]
    copies = [
        pltpu.make_async_copy(wo_ref, wov_ref, wsem.at[0]),
    ]
    for copy in copies:
        copy.start()
    deep = ndevs // 4
    slots, _, width = out_ref.shape
    nrows = ndevs * slots * 2
    hl = wov_ref.shape[0] // HD
    tiles = width // HD // pieces
    ob_ref[...] = o_ref[...]
    lb_ref[...] = l_ref[...]
    greet(ndevs)

    def finish_heads(mine, others):
        ls = [mine[1][...]] + [o[1][...] for o in others]
        top = functools.reduce(jnp.maximum, ls)
        es = [jnp.exp2(l - top) for l in ls]
        both = functools.reduce(jnp.add, es)
        refs = [mine[0]] + [o[0] for o in others]
        for span, got in weighted([(e / both, r) for e, r in zip(es, refs)]):
            head_ref[span] = got

    fold(ndevs, (ob_ref, lb_ref), (o1, l1), (o2, l2), (o3, l3),
         send.at[0], recv.at[0], merge_heads, finish_heads)
    heads = [head_ref[pl.ds(h, nrows, stride=hl), :].astype(BF) for h in range(hl)]
    head = jnp.concatenate(heads, axis=1)
    row = lax.broadcasted_iota(jnp.int32, (nrows, nrows), 0)
    col = lax.broadcasted_iota(jnp.int32, (nrows, nrows), 1)
    block = nrows // R
    source = row % block
    for j in range(R):
        source = source + jnp.where(row // block == j, place_ref[j] * block, 0)
    perm = jnp.where(col == source, 1.0, 0.0).astype(BF)
    head = jnp.dot(perm, head, preferred_element_type=F32).astype(BF)
    for copy in copies:
        copy.wait()
    for p in range(pieces):
        step = 8
        for t in range(0, tiles, step):
            at = (p * tiles + t) * HD
            got = jnp.dot(head, wov_ref[:, at:at + step * HD], preferred_element_type=F32)
            for i in range(step):
                wide_ref[pl.ds(t + i, nrows, stride=tiles), :] = got[:, i * HD:(i + 1) * HD]
        buf = sums[4 * p]
        buf[...] = wide_ref[...].astype(BF).reshape(buf.shape)

        def finish_sums(mine, others, p=p):
            total = mine[0][...].astype(F32)
            for o in others:
                total = total + o[0][...].astype(F32)
            wide_ref[:slots * 2 * tiles, :] = total
            for s in range(slots):
                for t in range(tiles):
                    at = (p * tiles + t) * HD
                    out_ref[s, :, at:at + HD] = (
                        wide_ref[pl.ds(s * 2 * tiles + t, 2, stride=tiles), :].astype(BF))

        fold(ndevs, (buf,), (sums[4 * p + 1],), (sums[4 * p + 2],), (sums[4 * p + 3],),
             send.at[1 + p], recv.at[1 + p], merge_sums, finish_sums)


def finish(o, lse, placement, wo, ndevs, slots, pieces=1):
    width = wo.shape[1]
    deep = ndevs // 4
    rows = o.shape[1]
    nrows = ndevs * slots * 2
    tall = slots * 2 * width // HD // pieces
    sizes = (ndevs, 2 * deep, deep, deep - 1)
    scratch = [pltpu.VMEM(o.shape, BF), pltpu.VMEM(lse.shape, F32)]
    for n in sizes[1:]:
        scratch += [pltpu.VMEM((n, rows, HD), BF), pltpu.VMEM((n,) + lse.shape[1:], F32)]
    scratch += [
        pltpu.VMEM(wo.shape, BF),
        pltpu.VMEM((rows, HD), F32),
        pltpu.VMEM((ndevs * tall, HD), F32),
    ]
    for _ in range(pieces):
        scratch += [pltpu.VMEM((n, tall, HD), BF) for n in sizes]
    sems = pltpu.SemaphoreType.DMA((1 + pieces, 8 * deep))
    scratch += [sems, sems, pltpu.SemaphoreType.DMA((1,))]
    return pl.pallas_call(
        functools.partial(finish_kernel, ndevs),
        out_shape=jax.ShapeDtypeStruct((slots, 2, width), BF),
        in_specs=[
            pl.BlockSpec(memory_space=pltpu.VMEM),
            pl.BlockSpec(memory_space=pltpu.VMEM),
            pl.BlockSpec(memory_space=pltpu.SMEM),
            pl.BlockSpec(memory_space=pl.ANY),
        ],
        out_specs=pl.BlockSpec(memory_space=pltpu.VMEM),
        scratch_shapes=scratch,
        compiler_params=pltpu.CompilerParams(
            collective_id=1, has_side_effects=True, vmem_limit_bytes=56 * 2 ** 20),
        name="finish",
    )(o, lse, placement, wo)


def local(hidden_in, latent_cache, lengths, placement, w_query, w_down, up_key, up_value, w_out):
    ndevs = lax.axis_size("xfer")
    rank = up_key.shape[0]
    hl = w_query.shape[1] // HD
    fw = w_down.shape[1]
    slot_rows = hidden_in.shape[0]
    samples = slot_rows * ndevs // R
    nrows = slot_rows * 2 * ndevs
    per = samples * 2 * hl
    both = project(hidden_in, w_query, w_down.T, ndevs)
    near = samples * 2
    request = jnp.minimum(lax.axis_index("xfer"), R - 1)
    own = lax.dynamic_slice_in_dim(both, nrows * hl + request * near, near, 1)[:, :, :fw]
    own = own.transpose(1, 0, 2).reshape(near, 2 * rank)
    own = jnp.pad(own, ((0, -near % 16), (0, 0)))
    o, lse = flash(both, own, latent_cache, lengths, up_key, up_value, hl, per)
    return finish(o, lse, placement, w_out, ndevs, slot_rows)


def solution(mesh):
    placed = (
        P(("parts", "xfer"), None, None),
        P("parts", "xfer", None),
        P("parts"),
        P("parts"),
        P(None, "xfer"),
        P(None, "xfer"),
        P(),
        P(),
        P("xfer", None),
    )
    return jax.shard_map(
        local,
        mesh=mesh,
        in_specs=placed,
        out_specs=P(("parts", "xfer"), None, None),
        check_vma=False,
    )
```

```python
import functools

import jax
import jax.numpy as jnp
from jax import lax
from jax.experimental import pallas as pl
from jax.experimental.pallas import tpu as pltpu
from jax.sharding import PartitionSpec as P

HEADS = 64
KVH = 8
HD = 128
R = 16
NEG = -1e30
LOG2E = 1.4426950408889634
BF = jnp.bfloat16
F32 = jnp.float32


def dot_nt(a, b):
    return lax.dot_general(a, b, (((1,), (1,)), ((), ())), preferred_element_type=F32)


def flash_kernel(hl, lengths_ref, both_ref, fresh_ref, cache_ref, upk_ref, upv_ref,
                 o_ref, lse_ref, hi_ref, lo_ref, lat_ref):
    ndevs = both_ref.shape[0]
    _, _, per, rank = hi_ref.shape
    rows = ndevs * per
    each = ndevs // KVH
    batch, positions, _ = cache_ref.shape
    step = pl.program_id(0)
    me = lax.axis_index("xfer")

    @pl.when(step == 0)
    def _():
        for g in range(KVH):
            qg = both_ref[g * each:(g + 1) * each, :R * per].reshape(each * R * per, HD)
            a = dot_nt(qg, upk_ref[:, g * HD:(g + 1) * HD])
            a = a * (HD ** -0.5 * LOG2E)
            hi = a.astype(BF)
            lo = (a - hi.astype(F32)).astype(BF)
            hi_ref[g * each:(g + 1) * each] = hi.reshape(each, R, per, rank)
            lo_ref[g * each:(g + 1) * each] = lo.reshape(each, R, per, rank)
        lse_ref[...] = jnp.zeros_like(lse_ref)

    lane = lax.broadcasted_iota(jnp.int32, (rows, HD), 1)

    def scores(req, keys):
        qh = hi_ref[:, pl.ds(req, 1)].reshape(rows, rank)
        ql = lo_ref[:, pl.ds(req, 1)].reshape(rows, rank)
        return dot_nt(qh, keys) + dot_nt(ql, keys)

    def weigh(s, vals):
        top = jnp.max(s, axis=1, keepdims=True)
        p = jnp.exp2(s - top)
        total = jnp.sum(p, axis=1, keepdims=True)
        acc = jnp.dot(p.astype(BF), vals, preferred_element_type=F32)
        return acc / total, top + jnp.log2(total)

    pos = lax.broadcasted_iota(jnp.int32, (rows, positions), 1)
    lses = lse_ref[...].reshape(rows, HD)
    ahead = scores(step * batch, cache_ref[0, :, :rank])
    for b in range(batch):
        req = step * batch + b
        s = ahead
        if b + 1 < batch:
            ahead = scores(req + 1, cache_ref[b + 1, :, :rank])
        s = jnp.where(pos < lengths_ref[req] - me * positions, s, NEG)
        out, lse = weigh(s, cache_ref[b, :, rank:])
        lat_ref[:, pl.ds(req, 1)] = out.astype(BF).reshape(ndevs, 1, per, rank)
        lses = jnp.where(lane == req, lse, lses)
    lse_ref[...] = lses.reshape(lse_ref.shape)

    @pl.when(me // batch == step)
    def _():
        n = scores(me, fresh_ref[:, :rank])
        row = lax.broadcasted_iota(jnp.int32, n.shape, 0) % per
        col = lax.broadcasted_iota(jnp.int32, n.shape, 1)
        rs, rt = row // (2 * hl), (row // hl) % 2
        n = jnp.where((rs == col // 2) & (col % 2 <= rt), n, NEG)
        near, near_lse = weigh(n, fresh_ref[:, rank:])
        lses = lse_ref[...].reshape(rows, HD)
        far_lse = jnp.sum(jnp.where(lane == me, lses, 0.0), axis=1, keepdims=True)
        far = lat_ref[:, pl.ds(me, 1)].reshape(rows, rank).astype(F32)
        top = jnp.maximum(near_lse, far_lse)
        en, ef = jnp.exp2(near_lse - top), jnp.exp2(far_lse - top)
        out = far + (en / (en + ef)) * (near - far)
        lat_ref[:, pl.ds(me, 1)] = out.astype(BF).reshape(ndevs, 1, per, rank)
        lse = top + jnp.log2(en + ef)
        lse_ref[...] = jnp.where(lane == me, lse, lses).reshape(lse_ref.shape)

    @pl.when(step == R // batch - 1)
    def _():
        for g in range(KVH):
            lg = lat_ref[g * each:(g + 1) * each].reshape(each * R * per, rank)
            o = jnp.dot(lg, upv_ref[:, g * HD:(g + 1) * HD], preferred_element_type=F32)
            o_ref[g * each:(g + 1) * each] = o.astype(BF).reshape(each, R * per, HD)


def flash(both, fresh, cache, lengths, upk, upv, hl, per, batch=4):
    ndevs = both.shape[0]
    rank = upv.shape[0]
    rows = ndevs * per
    positions = cache.shape[1]
    whole = lambda shape: pl.BlockSpec(shape, lambda i, *_: (0,) * len(shape))
    state = pltpu.VMEM((ndevs, R, per, rank), BF)
    return pl.pallas_call(
        functools.partial(flash_kernel, hl),
        out_shape=(
            jax.ShapeDtypeStruct((ndevs, R * per, HD), BF),
            jax.ShapeDtypeStruct((ndevs, per, HD), F32),
        ),
        grid_spec=pltpu.PrefetchScalarGridSpec(
            num_scalar_prefetch=1,
            grid=(R // batch,),
            in_specs=[
                whole(both.shape),
                whole(fresh.shape),
                pl.BlockSpec((batch, positions, 2 * rank), lambda i, *_: (i, 0, 0)),
                whole(upk.shape),
                whole(upv.shape),
            ],
            out_specs=[whole((ndevs, R * per, HD)), whole((ndevs, per, HD))],
            scratch_shapes=[state, state, state],
        ),
        compiler_params=pltpu.CompilerParams(vmem_limit_bytes=60 * 2 ** 20),
        cost_estimate=pl.CostEstimate(
            flops=2 * R * rows * positions * rank * 3,
            bytes_accessed=cache.size * 2,
            transcendentals=R * rows * positions,
        ),
        name="flash",
    )(lengths, both, fresh, cache, upk, upv)


def place(ndevs):
    me = lax.axis_index("xfer")
    return me // 4, (me // 2) % 2, me % 2


def index_of(z, y, c):
    return z * 4 + y * 2 + c


def greet(ndevs):
    deep = ndevs // 4
    z, y, c = place(ndevs)
    barrier = pltpu.get_barrier_semaphore()
    peers = [index_of((z + k) % deep, y, c) for k in range(1, deep)]
    peers += [index_of(z, 1 - y, c), index_of(z, y, 1 - c)]
    for peer in peers:
        pl.semaphore_signal(barrier, inc=1, device_id={"xfer": peer}, device_id_type=pl.DeviceIdType.MESH)
    pl.semaphore_wait(barrier, len(peers))


def remote(src, dst, send, recv, peer):
    return pltpu.make_async_remote_copy(
        src_ref=src, dst_ref=dst, send_sem=send, recv_sem=recv,
        device_id={"xfer": peer}, device_id_type=pl.DeviceIdType.MESH,
    )


def spread(ndevs, buf, send, recv):
    deep = ndevs // 4
    z, y, c = place(ndevs)
    far, near, twin = 0, deep, 2 * deep

    def move(block, slot, peer):
        return remote(buf.at[block], buf.at[block], send.at[slot], recv.at[slot], peer)

    mine = index_of(z, y, c)
    along = [move(mine, far + k, index_of((z + k) % deep, y, c)) for k in range(1, deep)]
    for copy in along:
        copy.start()
    across, over = [], []
    for k in range(deep + 1):
        if k:
            yield
        if k < deep:
            block = index_of((z - k + deep) % deep, y, c)
            if k:
                along[k - 1].wait_recv()
            across.append(move(block, near + k, index_of(z, 1 - y, c)))
            across[-1].start()
            over.append(move(block, twin + k, index_of(z, y, 1 - c)))
            over[-1].start()
        if k:
            across[k - 1].wait_recv()
            block = index_of((z - k + 1 + deep) % deep, 1 - y, c)
            over.append(move(block, twin + deep + k - 1, index_of(z, y, 1 - c)))
            over[-1].start()
    yield
    for copy in over:
        copy.wait_recv()
    for copy in along + across + over:
        copy.wait_send()


def drive(*works):
    works = list(works)
    while works:
        for work in list(works):
            if next(work, works) is works:
                works.remove(work)


def project_kernel(ndevs, hidden_ref, wq_ref, wd_ref, out_ref,
                   x_ref, wide_ref, wqv_ref, wdv_ref, stage_ref, send, recv, wsem):
    copies = [
        pltpu.make_async_copy(wq_ref, wqv_ref, wsem.at[0]),
        pltpu.make_async_copy(wd_ref, wdv_ref, wsem.at[1]),
    ]
    for copy in copies:
        copy.start()
    me = lax.axis_index("xfer")
    slots, _, width = hidden_ref.shape
    pieces = x_ref.shape[0]
    tiles = width // HD // pieces
    nrows = ndevs * slots * 2
    hl = wqv_ref.shape[1] // HD
    fw = wdv_ref.shape[0]
    for p in range(pieces):
        for s in range(slots):
            for t in range(tiles):
                at = (p * tiles + t) * HD
                wide_ref[pl.ds(s * 2 * tiles + t, 2, stride=tiles), :] = (
                    hidden_ref[s, :, at:at + HD].astype(F32))
        x_ref[p, pl.ds(me, 1)] = wide_ref[:slots * 2 * tiles, :].astype(BF)[None]
    greet(ndevs)
    sums = [jnp.zeros((nrows, hl * HD), F32), jnp.zeros((nrows, fw), F32)]

    def multiply(p, step=8):
        wide_ref[...] = x_ref[p].astype(F32).reshape(wide_ref.shape)
        for t in range(0, tiles, step):
            xt = jnp.concatenate(
                [wide_ref[pl.ds(t + i, nrows, stride=tiles), :].astype(BF) for i in range(step)], axis=1)
            span = slice((p * tiles + t) * HD, (p * tiles + t + step) * HD)
            sums[0] = sums[0] + jnp.dot(xt, wqv_ref[span], preferred_element_type=F32)
            sums[1] = sums[1] + dot_nt(xt, wdv_ref[:, span])
            yield

    gathers = [spread(ndevs, x_ref.at[p], send.at[p], recv.at[p]) for p in range(pieces)]
    for gather in gathers:
        next(gather)
    drive(gathers[0])
    for copy in copies:
        copy.wait()
    for p in range(pieces):
        drive(*gathers[p + 1:p + 2], multiply(p))
    query, fresh = sums
    for h in range(hl):
        stage_ref[pl.ds(h, nrows, stride=hl), :] = query[:, h * HD:(h + 1) * HD]
    for i in range(nrows // 16):
        stage_ref[nrows * hl:, i * fw:(i + 1) * fw] = fresh[i * 16:(i + 1) * 16]
    out_ref[pl.ds(me, 1)] = stage_ref[...].astype(BF)[None]
    drive(spread(ndevs, out_ref, send.at[pieces], recv.at[pieces]))


def project(hidden, wq, wd, ndevs, pieces=2):
    slots, _, width = hidden.shape
    tall = slots * 2 * width // HD // pieces
    nrows = ndevs * slots * 2
    hl = wq.shape[1] // HD
    sems = pltpu.SemaphoreType.DMA((pieces + 1, ndevs))
    return pl.pallas_call(
        functools.partial(project_kernel, ndevs),
        out_shape=jax.ShapeDtypeStruct((ndevs, nrows * hl + 16, HD), BF),
        in_specs=[
            pl.BlockSpec(memory_space=pltpu.VMEM),
            pl.BlockSpec(memory_space=pl.ANY),
            pl.BlockSpec(memory_space=pl.ANY),
        ],
        out_specs=pl.BlockSpec(memory_space=pltpu.VMEM),
        scratch_shapes=[
            pltpu.VMEM((pieces, ndevs, tall, HD), BF),
            pltpu.VMEM((ndevs * tall, HD), F32),
            pltpu.VMEM(wq.shape, BF),
            pltpu.VMEM(wd.shape, BF),
            pltpu.VMEM((nrows * hl + 16, HD), F32),
            sems, sems,
            pltpu.SemaphoreType.DMA((2,)),
        ],
        compiler_params=pltpu.CompilerParams(
            collective_id=0, has_side_effects=True, vmem_limit_bytes=56 * 2 ** 20),
        name="project",
    )(hidden, wq, wd)


def fold(ndevs, blocks, held1, held2, held3, send, recv, merge, finish):
    deep = ndevs // 4
    z, y, c = place(ndevs)
    many = len(blocks)
    at = lambda refs, i: [r.at[i] for r in refs]
    count = [0]

    def ship(src, dst, peer):
        copies = []
        for s, d in zip(src, dst):
            copies.append(remote(s, d, send.at[count[0]], recv.at[count[0]], peer))
            count[0] += 1
        for copy in copies:
            copy.start()
        return copies

    def arrive(copies):
        for copy in copies:
            copy.wait_recv()

    order = [(z + k) % deep for k in range(1, deep + 1)]
    twin = index_of(z, y, 1 - c)
    first = []
    for far in (1, 0):
        yy = 1 - y if far else y
        for k in range(deep):
            first.append(ship(at(blocks, index_of(order[k], yy, 1 - c)), at(held1, far * deep + k), twin))
    second = []
    for k in range(deep):
        yield
        arrive(first[k])
        here = at(blocks, index_of(order[k], 1 - y, c))
        merge(here, here, at(held1, deep + k))
        second.append(ship(here, at(held2, k), index_of(z, 1 - y, c)))
    for k in range(deep):
        yield
        arrive(first[deep + k])
        here = at(blocks, index_of(order[k], y, c))
        merge(here, here, at(held1, k))
    third = []
    for k in range(deep):
        yield
        arrive(second[k])
        here = at(blocks, index_of(order[k], y, c))
        merge(here, here, at(held2, k))
        if k < deep - 1:
            third.append(ship(here, at(held3, k), index_of(order[k], y, c)))
    yield
    for copies in third:
        arrive(copies)
    finish(at(blocks, index_of(z, y, c)), [at(held3, k) for k in range(deep - 1)])
    for copies in first + second + third:
        for copy in copies:
            copy.wait_send()


def weighted(terms):
    per = terms[0][0].shape[0]
    for req in range(R):
        span = slice(req * per, (req + 1) * per)
        got = None
        for share, block in terms:
            term = share[:, req:req + 1] * block[span].astype(F32)
            got = term if got is None else got + term
        yield span, got


def merge_heads(dst, a, b):
    la, lb = a[1][...], b[1][...]
    top = jnp.maximum(la, lb)
    ea, eb = jnp.exp2(la - top), jnp.exp2(lb - top)
    both = ea + eb
    for span, got in weighted([(ea / both, a[0]), (eb / both, b[0])]):
        dst[0][span] = got.astype(BF)
    dst[1][...] = top + jnp.log2(both)


def merge_sums(dst, a, b):
    dst[0][...] = (a[0][...].astype(F32) + b[0][...].astype(F32)).astype(BF)


def finish_kernel(ndevs, o_ref, l_ref, place_ref, wo_ref, out_ref,
                  ob_ref, lb_ref, o1, l1, o2, l2, o3, l3, wov_ref, head_ref, wide_ref, small_ref, *rest):
    pieces = (len(rest) - 3) // 4
    sums = rest[:4 * pieces]
    send, recv, wsem = rest[-3:]
    copies = [
        pltpu.make_async_copy(o_ref, ob_ref, wsem.at[0]),
        pltpu.make_async_copy(l_ref, lb_ref, wsem.at[1]),
        pltpu.make_async_copy(wo_ref, wov_ref, wsem.at[2]),
    ]
    for copy in copies:
        copy.start()
    deep = ndevs // 4
    slots, _, width = out_ref.shape
    nrows = ndevs * slots * 2
    hl = wov_ref.shape[0] // HD
    tiles = width // HD // pieces
    greet(ndevs)
    for copy in copies[:2]:
        copy.wait()

    def finish_heads(mine, others):
        ls = [mine[1][...]] + [o[1][...] for o in others]
        top = functools.reduce(jnp.maximum, ls)
        es = [jnp.exp2(l - top) for l in ls]
        both = functools.reduce(jnp.add, es)
        refs = [mine[0]] + [o[0] for o in others]
        for span, got in weighted([(e / both, r) for e, r in zip(es, refs)]):
            head_ref[span] = got

    drive(fold(ndevs, (ob_ref, lb_ref), (o1, l1), (o2, l2), (o3, l3),
               send.at[0], recv.at[0], merge_heads, finish_heads))
    heads = [head_ref[pl.ds(h, nrows, stride=hl), :].astype(BF) for h in range(hl)]
    head = jnp.concatenate(heads, axis=1)
    row = lax.broadcasted_iota(jnp.int32, (nrows, nrows), 0)
    col = lax.broadcasted_iota(jnp.int32, (nrows, nrows), 1)
    block = nrows // R
    source = row % block
    for j in range(R):
        source = source + jnp.where(row // block == j, place_ref[j] * block, 0)
    perm = jnp.where(col == source, 1.0, 0.0).astype(BF)
    head = jnp.dot(perm, head, preferred_element_type=F32).astype(BF)
    copies[2].wait()

    def multiply(p, step=8):
        for t in range(0, tiles, step):
            at = (p * tiles + t) * HD
            got = jnp.dot(head, wov_ref[:, at:at + step * HD], preferred_element_type=F32)
            for i in range(step):
                wide_ref[pl.ds(t + i, nrows, stride=tiles), :] = got[:, i * HD:(i + 1) * HD]
            yield
        sums[4 * p][...] = wide_ref[...].astype(BF).reshape(sums[4 * p].shape)

    def finish_sums(p, mine, others):
        total = mine[0][...].astype(F32)
        for o in others:
            total = total + o[0][...].astype(F32)
        small_ref[...] = total
        for s in range(slots):
            for t in range(tiles):
                at = (p * tiles + t) * HD
                out_ref[s, :, at:at + HD] = (
                    small_ref[pl.ds(s * 2 * tiles + t, 2, stride=tiles), :].astype(BF))

    folds = []
    for p in range(pieces):
        for _ in multiply(p):
            if folds:
                next(folds[-1])
        refs = sums[4 * p:4 * p + 4]
        folds.append(fold(ndevs, refs[:1], refs[1:2], refs[2:3], refs[3:],
                          send.at[1 + p], recv.at[1 + p], merge_sums, functools.partial(finish_sums, p)))
        next(folds[-1])
    drive(*folds)


def finish(o, lse, placement, wo, ndevs, slots, pieces=2):
    width = wo.shape[1]
    deep = ndevs // 4
    rows = o.shape[1]
    nrows = ndevs * slots * 2
    tall = slots * 2 * width // HD // pieces
    sizes = (ndevs, 2 * deep, deep, deep - 1)
    scratch = [pltpu.VMEM(o.shape, BF), pltpu.VMEM(lse.shape, F32)]
    for n in sizes[1:]:
        scratch += [pltpu.VMEM((n, rows, HD), BF), pltpu.VMEM((n,) + lse.shape[1:], F32)]
    scratch += [
        pltpu.VMEM(wo.shape, BF),
        pltpu.VMEM((rows, HD), F32),
        pltpu.VMEM((ndevs * tall, HD), F32),
        pltpu.VMEM((tall, HD), F32),
    ]
    for _ in range(pieces):
        scratch += [pltpu.VMEM((n, tall, HD), BF) for n in sizes]
    sems = pltpu.SemaphoreType.DMA((1 + pieces, 8 * deep))
    scratch += [sems, sems, pltpu.SemaphoreType.DMA((3,))]
    return pl.pallas_call(
        functools.partial(finish_kernel, ndevs),
        out_shape=jax.ShapeDtypeStruct((slots, 2, width), BF),
        in_specs=[
            pl.BlockSpec(memory_space=pl.ANY),
            pl.BlockSpec(memory_space=pl.ANY),
            pl.BlockSpec(memory_space=pltpu.SMEM),
            pl.BlockSpec(memory_space=pl.ANY),
        ],
        out_specs=pl.BlockSpec(memory_space=pltpu.VMEM),
        scratch_shapes=scratch,
        compiler_params=pltpu.CompilerParams(
            collective_id=1, has_side_effects=True, vmem_limit_bytes=56 * 2 ** 20),
        name="finish",
    )(o, lse, placement, wo)


def local(hidden_in, latent_cache, lengths, placement, w_query, w_down, up_key, up_value, w_out):
    ndevs = lax.axis_size("xfer")
    rank = up_key.shape[0]
    hl = w_query.shape[1] // HD
    fw = w_down.shape[1]
    slot_rows = hidden_in.shape[0]
    samples = slot_rows * ndevs // R
    nrows = slot_rows * 2 * ndevs
    per = samples * 2 * hl
    both = project(hidden_in, w_query, w_down.T, ndevs)
    near = samples * 2
    request = jnp.minimum(lax.axis_index("xfer"), R - 1)
    row = request * near
    own = lax.dynamic_slice(
        both, (0, nrows * hl + row % 16, row // 16 * fw), (ndevs, near, fw))
    own = own.transpose(1, 0, 2).reshape(near, 2 * rank)
    own = jnp.pad(own, ((0, -near % 16), (0, 0)))
    o, lse = flash(both, own, latent_cache, lengths, up_key, up_value, hl, per)
    return finish(o, lse, placement, w_out, ndevs, slot_rows)


def solution(mesh):
    placed = (
        P(("parts", "xfer"), None, None),
        P("parts", "xfer", None),
        P("parts"),
        P("parts"),
        P(None, "xfer"),
        P(None, "xfer"),
        P(),
        P(),
        P("xfer", None),
    )
    return jax.shard_map(
        local,
        mesh=mesh,
        in_specs=placed,
        out_specs=P(("parts", "xfer"), None, None),
        check_vma=False,
    )
```

```python
import functools

import jax
import jax.numpy as jnp
from jax import lax
from jax.experimental import pallas as pl
from jax.experimental.pallas import tpu as pltpu
from jax.sharding import PartitionSpec as P

HEADS = 64
KVH = 8
HD = 128
R = 16
NEG = -1e30
LOG2E = 1.4426950408889634
BF = jnp.bfloat16
F32 = jnp.float32


def dot_nt(a, b):
    return lax.dot_general(a, b, (((1,), (1,)), ((), ())), preferred_element_type=F32)


def flash_kernel(hl, lengths_ref, both_ref, fresh_ref, cache_ref, upk_ref, upv_ref,
                 o_ref, lse_ref, hi_ref, lo_ref, lat_ref):
    ndevs = both_ref.shape[0]
    _, _, per, rank = hi_ref.shape
    rows = ndevs * per
    each = ndevs // KVH
    batch, positions, _ = cache_ref.shape
    step = pl.program_id(0)
    me = lax.axis_index("xfer")

    @pl.when(step == 0)
    def _():
        for g in range(KVH):
            qg = both_ref[g * each:(g + 1) * each, :R * per].reshape(each * R * per, HD)
            a = dot_nt(qg, upk_ref[:, g * HD:(g + 1) * HD])
            a = a * (HD ** -0.5 * LOG2E)
            hi = a.astype(BF)
            lo = (a - hi.astype(F32)).astype(BF)
            hi_ref[g * each:(g + 1) * each] = hi.reshape(each, R, per, rank)
            lo_ref[g * each:(g + 1) * each] = lo.reshape(each, R, per, rank)
        lse_ref[...] = jnp.zeros_like(lse_ref)

    lane = lax.broadcasted_iota(jnp.int32, (rows, HD), 1)

    def scores(req, keys):
        qh = hi_ref[:, pl.ds(req, 1)].reshape(rows, rank)
        ql = lo_ref[:, pl.ds(req, 1)].reshape(rows, rank)
        return dot_nt(jnp.concatenate([qh, ql], axis=1), jnp.concatenate([keys, keys], axis=1))

    def weigh(s, vals):
        top = jnp.max(s, axis=1, keepdims=True)
        p = jnp.exp2(s - top)
        total = jnp.sum(p, axis=1, keepdims=True)
        acc = jnp.dot(p.astype(BF), vals, preferred_element_type=F32)
        return acc / total, top + jnp.log2(total)

    pos = lax.broadcasted_iota(jnp.int32, (rows, positions), 1)
    lses = lse_ref[...].reshape(rows, HD)
    ahead = scores(step * batch, cache_ref[0, :, :rank])
    for b in range(batch):
        req = step * batch + b
        s = ahead
        if b + 1 < batch:
            ahead = scores(req + 1, cache_ref[b + 1, :, :rank])
        s = jnp.where(pos < lengths_ref[req] - me * positions, s, NEG)
        out, lse = weigh(s, cache_ref[b, :, rank:])
        lat_ref[:, pl.ds(req, 1)] = out.astype(BF).reshape(ndevs, 1, per, rank)
        lses = jnp.where(lane == req, lse, lses)
    lse_ref[...] = lses.reshape(lse_ref.shape)

    @pl.when(me // batch == step)
    def _():
        n = scores(me, fresh_ref[:, :rank])
        row = lax.broadcasted_iota(jnp.int32, n.shape, 0) % per
        col = lax.broadcasted_iota(jnp.int32, n.shape, 1)
        rs, rt = row // (2 * hl), (row // hl) % 2
        n = jnp.where((rs == col // 2) & (col % 2 <= rt), n, NEG)
        near, near_lse = weigh(n, fresh_ref[:, rank:])
        lses = lse_ref[...].reshape(rows, HD)
        far_lse = jnp.sum(jnp.where(lane == me, lses, 0.0), axis=1, keepdims=True)
        far = lat_ref[:, pl.ds(me, 1)].reshape(rows, rank).astype(F32)
        top = jnp.maximum(near_lse, far_lse)
        en, ef = jnp.exp2(near_lse - top), jnp.exp2(far_lse - top)
        out = far + (en / (en + ef)) * (near - far)
        lat_ref[:, pl.ds(me, 1)] = out.astype(BF).reshape(ndevs, 1, per, rank)
        lse = top + jnp.log2(en + ef)
        lse_ref[...] = jnp.where(lane == me, lse, lses).reshape(lse_ref.shape)

    @pl.when(step == R // batch - 1)
    def _():
        for g in range(KVH):
            lg = lat_ref[g * each:(g + 1) * each].reshape(each * R * per, rank)
            o = jnp.dot(lg, upv_ref[:, g * HD:(g + 1) * HD], preferred_element_type=F32)
            o_ref[g * each:(g + 1) * each] = o.astype(BF).reshape(each, R * per, HD)


def flash(both, fresh, cache, lengths, upk, upv, hl, per, batch=4):
    ndevs = both.shape[0]
    rank = upv.shape[0]
    rows = ndevs * per
    positions = cache.shape[1]
    whole = lambda shape: pl.BlockSpec(shape, lambda i, *_: (0,) * len(shape))
    state = pltpu.VMEM((ndevs, R, per, rank), BF)
    return pl.pallas_call(
        functools.partial(flash_kernel, hl),
        out_shape=(
            jax.ShapeDtypeStruct((ndevs, R * per, HD), BF),
            jax.ShapeDtypeStruct((ndevs, per, HD), F32),
        ),
        grid_spec=pltpu.PrefetchScalarGridSpec(
            num_scalar_prefetch=1,
            grid=(R // batch,),
            in_specs=[
                whole(both.shape),
                whole(fresh.shape),
                pl.BlockSpec((batch, positions, 2 * rank), lambda i, *_: (i, 0, 0)),
                whole(upk.shape),
                whole(upv.shape),
            ],
            out_specs=[whole((ndevs, R * per, HD)), whole((ndevs, per, HD))],
            scratch_shapes=[state, state, state],
        ),
        compiler_params=pltpu.CompilerParams(vmem_limit_bytes=60 * 2 ** 20),
        cost_estimate=pl.CostEstimate(
            flops=2 * R * rows * positions * rank * 3,
            bytes_accessed=cache.size * 2,
            transcendentals=R * rows * positions,
        ),
        name="flash",
    )(lengths, both, fresh, cache, upk, upv)


def place(ndevs):
    me = lax.axis_index("xfer")
    return me // 4, (me // 2) % 2, me % 2


def index_of(z, y, c):
    return z * 4 + y * 2 + c


def greet(ndevs):
    deep = ndevs // 4
    z, y, c = place(ndevs)
    barrier = pltpu.get_barrier_semaphore()
    peers = [index_of((z + k) % deep, y, c) for k in range(1, deep)]
    peers += [index_of(z, 1 - y, c), index_of(z, y, 1 - c)]
    for peer in peers:
        pl.semaphore_signal(barrier, inc=1, device_id={"xfer": peer}, device_id_type=pl.DeviceIdType.MESH)
    pl.semaphore_wait(barrier, len(peers))


def remote(src, dst, send, recv, peer):
    return pltpu.make_async_remote_copy(
        src_ref=src, dst_ref=dst, send_sem=send, recv_sem=recv,
        device_id={"xfer": peer}, device_id_type=pl.DeviceIdType.MESH,
    )


def spread(ndevs, buf, send, recv):
    deep = ndevs // 4
    z, y, c = place(ndevs)
    far, near, twin = 0, deep, 2 * deep

    def move(block, slot, peer):
        return remote(buf.at[block], buf.at[block], send.at[slot], recv.at[slot], peer)

    mine = index_of(z, y, c)
    along = [move(mine, far + k, index_of((z + k) % deep, y, c)) for k in range(1, deep)]
    for copy in along:
        copy.start()
    across, over = [], []
    for k in range(deep + 1):
        if k:
            yield
        if k < deep:
            block = index_of((z - k + deep) % deep, y, c)
            if k:
                along[k - 1].wait_recv()
            across.append(move(block, near + k, index_of(z, 1 - y, c)))
            across[-1].start()
            over.append(move(block, twin + k, index_of(z, y, 1 - c)))
            over[-1].start()
        if k:
            across[k - 1].wait_recv()
            block = index_of((z - k + 1 + deep) % deep, 1 - y, c)
            over.append(move(block, twin + deep + k - 1, index_of(z, y, 1 - c)))
            over[-1].start()
    yield
    for copy in over:
        copy.wait_recv()
    for copy in along + across + over:
        copy.wait_send()


def drive(*works):
    works = list(works)
    while works:
        for work in list(works):
            if next(work, works) is works:
                works.remove(work)


def project_kernel(ndevs, hidden_ref, wq_ref, wd_ref, out_ref,
                   x_ref, wide_ref, wqv_ref, wdv_ref, stage_ref, send, recv, wsem):
    copies = [
        pltpu.make_async_copy(wq_ref, wqv_ref, wsem.at[0]),
        pltpu.make_async_copy(wd_ref, wdv_ref, wsem.at[1]),
    ]
    for copy in copies:
        copy.start()
    me = lax.axis_index("xfer")
    slots, _, width = hidden_ref.shape
    pieces = x_ref.shape[0]
    tiles = width // HD // pieces
    nrows = ndevs * slots * 2
    hl = wqv_ref.shape[1] // HD
    fw = wdv_ref.shape[0]
    for p in range(pieces):
        for s in range(slots):
            for t in range(tiles):
                at = (p * tiles + t) * HD
                wide_ref[pl.ds(s * 2 * tiles + t, 2, stride=tiles), :] = (
                    hidden_ref[s, :, at:at + HD].astype(F32))
        x_ref[p, pl.ds(me, 1)] = wide_ref[:slots * 2 * tiles, :].astype(BF)[None]
    greet(ndevs)
    sums = [jnp.zeros((nrows, hl * HD), F32), jnp.zeros((nrows, fw), F32)]

    def multiply(p, step=16):
        wide_ref[...] = x_ref[p].astype(F32).reshape(wide_ref.shape)
        for t in range(0, tiles, step):
            xt = jnp.concatenate(
                [wide_ref[pl.ds(t + i, nrows, stride=tiles), :].astype(BF) for i in range(step)], axis=1)
            span = slice((p * tiles + t) * HD, (p * tiles + t + step) * HD)
            sums[0] = sums[0] + jnp.dot(xt, wqv_ref[span], preferred_element_type=F32)
            sums[1] = sums[1] + dot_nt(xt, wdv_ref[:, span])
            yield

    gathers = [spread(ndevs, x_ref.at[p], send.at[p], recv.at[p]) for p in range(pieces)]
    for gather in gathers:
        next(gather)
    drive(gathers[0])
    for copy in copies:
        copy.wait()
    for p in range(pieces):
        drive(*gathers[p + 1:p + 2], multiply(p))
    query, fresh = sums
    for h in range(hl):
        stage_ref[pl.ds(h, nrows, stride=hl), :] = query[:, h * HD:(h + 1) * HD]
    for i in range(nrows // 16):
        stage_ref[nrows * hl:, i * fw:(i + 1) * fw] = fresh[i * 16:(i + 1) * 16]
    out_ref[pl.ds(me, 1)] = stage_ref[...].astype(BF)[None]
    drive(spread(ndevs, out_ref, send.at[pieces], recv.at[pieces]))


def project(hidden, wq, wd, ndevs, pieces=1):
    slots, _, width = hidden.shape
    tall = slots * 2 * width // HD // pieces
    nrows = ndevs * slots * 2
    hl = wq.shape[1] // HD
    sems = pltpu.SemaphoreType.DMA((pieces + 1, ndevs))
    return pl.pallas_call(
        functools.partial(project_kernel, ndevs),
        out_shape=jax.ShapeDtypeStruct((ndevs, nrows * hl + 16, HD), BF),
        in_specs=[
            pl.BlockSpec(memory_space=pltpu.VMEM),
            pl.BlockSpec(memory_space=pl.ANY),
            pl.BlockSpec(memory_space=pl.ANY),
        ],
        out_specs=pl.BlockSpec(memory_space=pltpu.VMEM),
        scratch_shapes=[
            pltpu.VMEM((pieces, ndevs, tall, HD), BF),
            pltpu.VMEM((ndevs * tall, HD), F32),
            pltpu.VMEM(wq.shape, BF),
            pltpu.VMEM(wd.shape, BF),
            pltpu.VMEM((nrows * hl + 16, HD), F32),
            sems, sems,
            pltpu.SemaphoreType.DMA((2,)),
        ],
        compiler_params=pltpu.CompilerParams(
            collective_id=0, has_side_effects=True, vmem_limit_bytes=56 * 2 ** 20),
        name="project",
    )(hidden, wq, wd)


def fold(ndevs, blocks, held1, held2, held3, send, recv, merge, finish):
    deep = ndevs // 4
    z, y, c = place(ndevs)
    many = len(blocks)
    at = lambda refs, i: [r.at[i] for r in refs]
    count = [0]

    def ship(src, dst, peer):
        copies = []
        for s, d in zip(src, dst):
            copies.append(remote(s, d, send.at[count[0]], recv.at[count[0]], peer))
            count[0] += 1
        for copy in copies:
            copy.start()
        return copies

    def arrive(copies):
        for copy in copies:
            copy.wait_recv()

    order = [(z + k) % deep for k in range(1, deep + 1)]
    twin = index_of(z, y, 1 - c)
    first = []
    for far in (1, 0):
        yy = 1 - y if far else y
        for k in range(deep):
            first.append(ship(at(blocks, index_of(order[k], yy, 1 - c)), at(held1, far * deep + k), twin))
    second = []
    for k in range(deep):
        yield
        arrive(first[k])
        here = at(blocks, index_of(order[k], 1 - y, c))
        merge(here, here, at(held1, deep + k))
        second.append(ship(here, at(held2, k), index_of(z, 1 - y, c)))
    for k in range(deep):
        yield
        arrive(first[deep + k])
        here = at(blocks, index_of(order[k], y, c))
        merge(here, here, at(held1, k))
    third = []
    for k in range(deep):
        yield
        arrive(second[k])
        here = at(blocks, index_of(order[k], y, c))
        merge(here, here, at(held2, k))
        if k < deep - 1:
            third.append(ship(here, at(held3, k), index_of(order[k], y, c)))
    yield
    for copies in third:
        arrive(copies)
    finish(at(blocks, index_of(z, y, c)), [at(held3, k) for k in range(deep - 1)])
    for copies in first + second + third:
        for copy in copies:
            copy.wait_send()


def weighted(terms):
    per = terms[0][0].shape[0]
    for req in range(R):
        span = slice(req * per, (req + 1) * per)
        got = None
        for share, block in terms:
            term = share[:, req:req + 1] * block[span].astype(F32)
            got = term if got is None else got + term
        yield span, got


def merge_heads(dst, a, b):
    la, lb = a[1][...], b[1][...]
    top = jnp.maximum(la, lb)
    ea, eb = jnp.exp2(la - top), jnp.exp2(lb - top)
    both = ea + eb
    for span, got in weighted([(ea / both, a[0]), (eb / both, b[0])]):
        dst[0][span] = got.astype(BF)
    dst[1][...] = top + jnp.log2(both)


def merge_sums(dst, a, b):
    dst[0][...] = (a[0][...].astype(F32) + b[0][...].astype(F32)).astype(BF)


def finish_kernel(ndevs, o_ref, l_ref, place_ref, wo_ref, out_ref,
                  ob_ref, lb_ref, o1, l1, o2, l2, o3, l3, wov_ref, head_ref, wide_ref, small_ref, *rest):
    pieces = (len(rest) - 3) // 4
    sums = rest[:4 * pieces]
    send, recv, wsem = rest[-3:]
    copies = [
        pltpu.make_async_copy(o_ref, ob_ref, wsem.at[0]),
        pltpu.make_async_copy(l_ref, lb_ref, wsem.at[1]),
        pltpu.make_async_copy(wo_ref, wov_ref, wsem.at[2]),
    ]
    for copy in copies:
        copy.start()
    deep = ndevs // 4
    slots, _, width = out_ref.shape
    nrows = ndevs * slots * 2
    hl = wov_ref.shape[0] // HD
    tiles = width // HD // pieces
    greet(ndevs)
    for copy in copies[:2]:
        copy.wait()

    def finish_heads(mine, others):
        ls = [mine[1][...]] + [o[1][...] for o in others]
        top = functools.reduce(jnp.maximum, ls)
        es = [jnp.exp2(l - top) for l in ls]
        both = functools.reduce(jnp.add, es)
        refs = [mine[0]] + [o[0] for o in others]
        for span, got in weighted([(e / both, r) for e, r in zip(es, refs)]):
            head_ref[span] = got

    drive(fold(ndevs, (ob_ref, lb_ref), (o1, l1), (o2, l2), (o3, l3),
               send.at[0], recv.at[0], merge_heads, finish_heads))
    heads = [head_ref[pl.ds(h, nrows, stride=hl), :].astype(BF) for h in range(hl)]
    head = jnp.concatenate(heads, axis=1)
    row = lax.broadcasted_iota(jnp.int32, (nrows, nrows), 0)
    col = lax.broadcasted_iota(jnp.int32, (nrows, nrows), 1)
    block = nrows // R
    source = row % block
    for j in range(R):
        source = source + jnp.where(row // block == j, place_ref[j] * block, 0)
    perm = jnp.where(col == source, 1.0, 0.0).astype(BF)
    head = jnp.dot(perm, head, preferred_element_type=F32).astype(BF)
    copies[2].wait()

    def multiply(p, step=8):
        for t in range(0, tiles, step):
            at = (p * tiles + t) * HD
            got = jnp.dot(head, wov_ref[:, at:at + step * HD], preferred_element_type=F32)
            for i in range(step):
                wide_ref[pl.ds(t + i, nrows, stride=tiles), :] = got[:, i * HD:(i + 1) * HD]
            yield
        sums[4 * p][...] = wide_ref[...].astype(BF).reshape(sums[4 * p].shape)

    def finish_sums(p, mine, others):
        total = mine[0][...].astype(F32)
        for o in others:
            total = total + o[0][...].astype(F32)
        small_ref[...] = total
        for s in range(slots):
            for t in range(tiles):
                at = (p * tiles + t) * HD
                out_ref[s, :, at:at + HD] = (
                    small_ref[pl.ds(s * 2 * tiles + t, 2, stride=tiles), :])

    folds = []
    for p in range(pieces):
        for _ in multiply(p):
            if folds:
                next(folds[-1])
        refs = sums[4 * p:4 * p + 4]
        folds.append(fold(ndevs, refs[:1], refs[1:2], refs[2:3], refs[3:],
                          send.at[1 + p], recv.at[1 + p], merge_sums, functools.partial(finish_sums, p)))
        next(folds[-1])
    drive(*folds)


def finish(o, lse, placement, wo, ndevs, slots, pieces=1):
    width = wo.shape[1]
    deep = ndevs // 4
    rows = o.shape[1]
    nrows = ndevs * slots * 2
    tall = slots * 2 * width // HD // pieces
    sizes = (ndevs, 2 * deep, deep, deep - 1)
    scratch = [pltpu.VMEM(o.shape, BF), pltpu.VMEM(lse.shape, F32)]
    for n in sizes[1:]:
        scratch += [pltpu.VMEM((n, rows, HD), BF), pltpu.VMEM((n,) + lse.shape[1:], F32)]
    scratch += [
        pltpu.VMEM(wo.shape, BF),
        pltpu.VMEM((rows, HD), F32),
        pltpu.VMEM((ndevs * tall, HD), F32),
        pltpu.VMEM((tall, HD), F32),
    ]
    for _ in range(pieces):
        scratch += [pltpu.VMEM((n, tall, HD), BF) for n in sizes]
    sems = pltpu.SemaphoreType.DMA((1 + pieces, 8 * deep))
    scratch += [sems, sems, pltpu.SemaphoreType.DMA((3,))]
    return pl.pallas_call(
        functools.partial(finish_kernel, ndevs),
        out_shape=jax.ShapeDtypeStruct((slots, 2, width), F32),
        in_specs=[
            pl.BlockSpec(memory_space=pl.ANY),
            pl.BlockSpec(memory_space=pl.ANY),
            pl.BlockSpec(memory_space=pltpu.SMEM),
            pl.BlockSpec(memory_space=pl.ANY),
        ],
        out_specs=pl.BlockSpec(memory_space=pltpu.VMEM),
        scratch_shapes=scratch,
        compiler_params=pltpu.CompilerParams(
            collective_id=1, has_side_effects=True, vmem_limit_bytes=56 * 2 ** 20),
        name="finish",
    )(o, lse, placement, wo)


def local(hidden_in, latent_cache, lengths, placement, w_query, w_down, up_key, up_value, w_out):
    ndevs = lax.axis_size("xfer")
    rank = up_key.shape[0]
    hl = w_query.shape[1] // HD
    fw = w_down.shape[1]
    slot_rows = hidden_in.shape[0]
    samples = slot_rows * ndevs // R
    nrows = slot_rows * 2 * ndevs
    per = samples * 2 * hl
    both = project(hidden_in, w_query, w_down.T, ndevs)
    near = samples * 2
    request = jnp.minimum(lax.axis_index("xfer"), R - 1)
    row = request * near
    own = lax.dynamic_slice(
        both, (0, nrows * hl + row % 16, row // 16 * fw), (ndevs, near, fw))
    own = own.transpose(1, 0, 2).reshape(near, 2 * rank)
    o, lse = flash(both, own, latent_cache, lengths, up_key, up_value, hl, per)
    return finish(o, lse, placement, w_out, ndevs, slot_rows).astype(BF)


def solution(mesh):
    placed = (
        P(("parts", "xfer"), None, None),
        P("parts", "xfer", None),
        P("parts"),
        P("parts"),
        P(None, "xfer"),
        P(None, "xfer"),
        P(),
        P(),
        P("xfer", None),
    )
    return jax.shard_map(
        local,
        mesh=mesh,
        in_specs=placed,
        out_specs=P(("parts", "xfer"), None, None),
        check_vma=False,
    )
```
